512 devices in a mesh: row: 32 (over z, y_lo), col: 16 (over y_hi, x, core).
Axes of the slice: x: 4, y: 8 (y_hi: 2, y_lo: 4; y = y_hi * 4 + y_lo), z: 8, core: 2. Of those that a mesh axis runs over, the one named last changes fastest.
Arguments:
- image_emb: bfloat16 [12288, 1024], P(('row', 'col')), may hold values from -8 to 8
- text_emb: bfloat16 [12288, 1024], P(('row', 'col')), may hold values from -8 to 8
- groups: int32 [12288], P(('row', 'col')), may hold values from 0 to 3071
- hidden: bfloat16 [12288, 1280], P('row'), may hold values from -6 to 6
- gain: float32 [1280], replicated, may hold values from 0.25 to 1.75
- w_in: bfloat16 [1280, 5120], P(None, 'col'), may hold values from -0.15625 to 0.15625
- w_out: bfloat16 [5120, 1280], P('col'), may hold values from -0.078125 to 0.078125
- w_proj: bfloat16 [1280, 1024], P('col'), may hold values from -0.15625 to 0.15625
Outputs:
- grad_image: bfloat16 [12288, 1024], P(('row', 'col'))
- grad_hidden: bfloat16 [12288, 1280], P('row')
The draws below stay inside these ranges and needn't reach their ends.
All inputs are finite; a program needn't handle non-finite values.
Results may differ from the reference program's by a relative error of at most 0.034.
Values may be sent and summed in bfloat16 or wider, within the bound.
A program may use at most 64 MiB of HBM per device.

```python
import jax
import jax.numpy as jnp
from jax import lax

E = 1024
D = 1280
FF = 5120
PAIR_DEV = 24
PAIRS = 12288
N_ROW = 32
N_COL = 16


def aligned_rows(key):
    signs = jnp.where(jax.random.bernoulli(jax.random.fold_in(key, 101), 0.5, (8, E)), 1.0, -1.0)
    target = 110.0 + 20.0 * jnp.arange(8, dtype=jnp.float32)
    strength = jnp.sqrt(8.0 * target / E)
    return (signs * strength[:, None], target)


def drawn_places():
    return (jnp.arange(8) * (PAIRS // 8) + 3) % PAIRS


def draw_image_emb(key, part):
    anchor = key
    key = jax.random.fold_in(key, 1)
    pattern, target = aligned_rows(anchor)
    values = jnp.clip(jax.random.normal(key, (PAIRS, E), jnp.float32), -4.0, 4.0)
    values = values.at[drawn_places()].set(pattern)
    return values.astype(jnp.bfloat16)


def draw_text_emb(key, part):
    anchor = key
    key = jax.random.fold_in(key, 2)
    pattern, target = aligned_rows(anchor)
    lowered = pattern * (1.0 - 2.0 / target)[:, None]
    values = jnp.clip(jax.random.normal(key, (PAIRS, E), jnp.float32), -4.0, 4.0)
    places = drawn_places()
    values = values.at[(places + PAIRS // 2 + 5) % PAIRS].set(pattern)
    values = values.at[(places + PAIRS // 2 + 6) % PAIRS].set(lowered)
    return values.astype(jnp.bfloat16)


def draw_groups(key, part):
    key = jax.random.fold_in(key, 7)
    first_key, second_key = jax.random.split(key)
    labels = jax.random.randint(first_key, (PAIRS,), 0, PAIRS // 4, jnp.int32)
    place = jax.random.randint(second_key, (), 0, PAIRS, jnp.int32)
    return labels.at[place].set(PAIRS // 4 - 1)


def levels(rng, shape, cuts, least, top_value):
    factor_of = 1.0
    for dim, blocks in cuts:
        steps = jax.random.uniform(jax.random.fold_in(jax.random.fold_in(rng, 6), dim), (blocks,), jnp.float32, least / len(cuts), top_value / len(cuts))
        factor_of = factor_of * jnp.repeat(jnp.exp(steps), shape[dim] // blocks).reshape((-1,) + (1,) * (len(shape) - 1 - dim))
    return factor_of


def scatter_about(own_key, extent, scale, bound, pieces=(), held_as=jnp.bfloat16):
    array = jax.random.normal(own_key, extent, jnp.float32) * scale
    if len(pieces) > 0:
        array = levels(own_key, extent, pieces, -0.22, 0.18) * array
    return jnp.clip(array, min=-bound, max=bound).astype(held_as)


def setup_inputs(seed: int = 0) -> dict:
    streams_of = jax.random.split(jax.random.key(seed), 9)
    image_emb = draw_image_emb(jax.random.fold_in(streams_of[8], 71), 0)
    text_emb = draw_text_emb(jax.random.fold_in(streams_of[8], 71), 0)
    groups = draw_groups(jax.random.fold_in(streams_of[8], 71), 0)
    hidden = scatter_about(streams_of[3], (PAIRS, D), 1.0, 6.0, ((0, 32),))
    gain = jnp.clip(1.0 + 0.15 * jax.random.normal(streams_of[4], (D,), jnp.float32), 0.25, 1.75)
    w_in = scatter_about(streams_of[5], (D, FF), D ** -0.5, 0.15625, ((1, 16),))
    w_out = scatter_about(streams_of[6], (FF, D), FF ** -0.5, 0.078125, ((0, 16),))
    w_proj = scatter_about(streams_of[7], (D, E), D ** -0.5, 0.15625, ((0, 16),))
    return dict(image_emb=image_emb, text_emb=text_emb, groups=groups, hidden=hidden, gain=gain, w_in=w_in, w_out=w_out, w_proj=w_proj)


logit_scale = 0.125
eps = 1e-05

def reference(image_emb, text_emb, groups, hidden, gain, w_in, w_out, w_proj):
    block_rows = PAIRS // N_ROW
    image_blocks = image_emb.reshape(N_ROW, block_rows, E)
    group_blocks = groups.reshape(N_ROW, block_rows)

    def scores_of(block):
        return logit_scale * jnp.dot(block, text_emb.T, preferred_element_type=jnp.float32)

    def first_pass(carry, inputs):
        col_peak, col_total, col_count = carry
        block, group_block = inputs
        scores = scores_of(block)
        positive = (group_block[:, None] == groups[None, :]).astype(jnp.float32)
        row_peak = lax.optimization_barrier(jnp.max(scores, axis=1))
        row_total = lax.optimization_barrier(jnp.sum(jnp.exp(scores - row_peak[:, None]), axis=1))
        row_lse = row_peak + jnp.log(row_total)
        row_count = lax.optimization_barrier(jnp.sum(positive, axis=1))
        new_peak = jnp.maximum(col_peak, lax.optimization_barrier(jnp.max(scores, axis=0)))
        col_total = col_total * jnp.exp(col_peak - new_peak) + lax.optimization_barrier(jnp.sum(jnp.exp(scores - new_peak[None, :]), axis=0))
        col_count = col_count + lax.optimization_barrier(jnp.sum(positive, axis=0))
        return ((new_peak, col_total, col_count), (row_lse, row_count))
    start = (jnp.full((PAIRS,), -1e+30, jnp.float32), jnp.zeros((PAIRS,), jnp.float32), jnp.zeros((PAIRS,), jnp.float32))
    (col_peak, col_total, col_count), (row_lse, row_count) = lax.scan(first_pass, start, (image_blocks, group_blocks))
    col_lse = col_peak + jnp.log(col_total)
    text_tiles = text_emb.astype(jnp.float32).reshape(N_ROW, N_COL, PAIR_DEV, E)

    def second_pass(accum, inputs):
        block, group_block, lse_block, count_block = inputs
        scores = scores_of(block)
        positive = (group_block[:, None] == groups[None, :]).astype(jnp.float32)
        dscore = 0.5 * (jnp.exp(scores - lse_block[:, None]) + jnp.exp(scores - col_lse[None, :]) - positive * (1.0 / count_block[:, None] + 1.0 / col_count[None, :]))
        dscore = dscore.astype(jnp.bfloat16)
        tiled = dscore.astype(jnp.float32).reshape(block_rows, N_ROW, N_COL, PAIR_DEV)
        partial_image = logit_scale * jnp.einsum('brck,rcke->bce', tiled, text_tiles)
        partial_image = partial_image.astype(jnp.bfloat16).astype(jnp.float32)
        image_grad = lax.optimization_barrier(jnp.sum(partial_image, axis=1)).astype(jnp.bfloat16)
        partial_text = logit_scale * jnp.dot(dscore.T, block, preferred_element_type=jnp.float32)
        accum = accum + partial_text.astype(jnp.bfloat16).astype(jnp.float32)
        return (accum, image_grad)
    accum, image_grads = lax.scan(second_pass, jnp.zeros((PAIRS, E), jnp.float32), (image_blocks, group_blocks, row_lse, row_count))
    grad_image = image_grads.reshape(PAIRS, E)
    grad_text = accum.astype(jnp.bfloat16)
    states = hidden.astype(jnp.float32)
    centered = states - lax.optimization_barrier(jnp.mean(states, axis=1, keepdims=True))
    rstd = lax.rsqrt(lax.optimization_barrier(jnp.mean(centered * centered, axis=1, keepdims=True)) + eps)
    normed = centered * rstd
    inner = (normed * gain[None, :]).astype(jnp.bfloat16)
    act = jnp.dot(inner, w_in, preferred_element_type=jnp.float32)
    slope = 0.5 * (1.0 + jax.scipy.special.erf(act * 0.7071067811865476)) + act * jnp.exp(-0.5 * act * act) * 0.3989422804014327
    dy_full = jnp.dot(grad_text, w_proj.T, preferred_element_type=jnp.float32).astype(jnp.bfloat16)
    dact = (jnp.dot(dy_full, w_out.T, preferred_element_type=jnp.float32) * slope).astype(jnp.bfloat16)
    unit_block = FF // N_COL
    dact_blocks = jnp.moveaxis(dact.reshape(PAIRS, N_COL, unit_block), 1, 0)
    weight_blocks = jnp.moveaxis(w_in.reshape(D, N_COL, unit_block), 1, 0)

    def add_block(total, inputs):
        dact_block, weight_block = inputs
        partial_sum = lax.dot_general(dact_block, weight_block, (((1,), (1,)), ((), ())), preferred_element_type=jnp.float32)
        rounded = lax.optimization_barrier(partial_sum.astype(jnp.bfloat16))
        return (total + rounded.astype(jnp.float32), None)
    dinner, _ = lax.scan(add_block, jnp.zeros((PAIRS, D), jnp.float32), (dact_blocks, weight_blocks))
    scaled = dinner * gain[None, :]
    back = rstd * (scaled - lax.optimization_barrier(jnp.mean(scaled, axis=1, keepdims=True)) - normed * lax.optimization_barrier(jnp.mean(scaled * normed, axis=1, keepdims=True)))
    grad_hidden = (dy_full.astype(jnp.float32) + back).astype(jnp.bfloat16)
    return (grad_image, grad_hidden)
```

```python
import jax
import jax.numpy as jnp
from jax import lax
from jax.experimental import pallas as pl
from jax.experimental.pallas import tpu as pltpu
from jax.sharding import PartitionSpec as P

MESH = pl.DeviceIdType.MESH
bf16, f32 = jnp.bfloat16, jnp.float32
logit_scale = 0.125
eps = 1e-05
E, D, FB = 1024, 1280, 320
EX = E + 128
R2 = 48
N_MSG = 160


def device(x, y, z, c):
    x, y, z = lax.rem(x + 4, 4), lax.rem(y + 8, 8), lax.rem(z + 8, 8)
    return (z * 4 + lax.rem(y, 4), (lax.div(y, 4) * 4 + x) * 2 + c)


def rows(block, size=R2):
    return pl.ds(pl.multiple_of(block * size, 16), size)


class Net:
    def __init__(self, send_sem, recv_sem):
        self.send_sem, self.recv_sem, self.count, self.sent = send_sem, recv_sem, 0, []

    def make(self, src, dst, target):
        copy = pltpu.make_async_remote_copy(
            src_ref=src,
            dst_ref=dst,
            send_sem=self.send_sem.at[self.count],
            recv_sem=self.recv_sem.at[self.count],
            device_id=target,
            device_id_type=MESH,
        )
        self.count += 1
        return copy

    def send(self, src, dst, target):
        copy = self.make(src, dst, target)
        copy.start()
        self.sent.append(copy)
        return copy

    def finish(self):
        for copy in self.sent:
            copy.wait_send()


def nt(a, b):
    return lax.dot_general(a, b, (((1,), (1,)), ((), ())), preferred_element_type=f32)


def tn(a, b):
    return lax.dot_general(a, b, (((0,), (0,)), ((), ())), preferred_element_type=f32)


def nn(a, b):
    return jnp.dot(a, b, preferred_element_type=f32)


def log_sum_exp(parts):
    peak = parts[0]
    for part in parts[1:]:
        peak = jnp.maximum(peak, part)
    total = jnp.exp(parts[0] - peak)
    for part in parts[1:]:
        total = total + jnp.exp(part - peak)
    return peak + jnp.log(total)


def kernel(
    img_in, txt_in, grp, hid, gain, w_in, w_out, w_proj,
    gi_out, gh_out,
    pair_out, pair_in, both,
    img, txt, sc, pos, row_stat, ds, gi, gt, gt_sib,
    rs_out, rs_in, fin, pr_out, pr_in,
    st_r, st_c, sl_r, sl_c, st_r2, st_c2, sl_r2, sl_c2, row_b,
    slots, gtf, wp, dy, slope, part, part_sib, q_out, q_in, y_out, y_in,
    send_sem, recv_sem,
):
    row, col = lax.axis_index("row"), lax.axis_index("col")
    z, yl = lax.div(row, 4), lax.rem(row, 4)
    yh, c = lax.div(col, 8), lax.rem(col, 2)
    x = lax.rem(lax.div(col, 2), 4)
    y = yh * 4 + yl
    xt = x + 1 - 2 * lax.rem(x, 2)
    xi = 3 - x
    at_t, at_i = lax.rem(x, 2), lax.div(x, 2)
    sib = device(x, y, z, 1 - c)
    part_t, part_i = device(xt, y, z, c), device(xi, y, z, c)
    part_t_sib = device(xt, y, z, 1 - c)
    y_of = [device(x, y + i, z, c) for i in range(8)]
    z_of = [device(x, y, z + i, c) for i in range(8)]
    x_of = [device(x + i, y, z, c) for i in range(4)]
    net = Net(send_sem, recv_sem)

    barrier = pltpu.get_barrier_semaphore()
    friends = y_of[1:] + z_of[1:] + x_of[1:] + [sib, part_t_sib]
    for friend in friends:
        pl.semaphore_signal(barrier, inc=1, device_id=friend, device_id_type=MESH)

    lane = lax.broadcasted_iota(jnp.int32, (24, 128), 1)
    ids = grp[...]
    hit = (lane == lax.shift_right_logical(ids, 6)) | (lane == (ids & 63) + 64)
    digits = jnp.where(hit, 1.0, 0.0).astype(f32)
    own = []
    for s, ref in ((0, img_in), (1, txt_in)):
        value = jnp.concatenate([ref[...].astype(f32), digits], axis=1)
        own.append(value)
        second = jnp.concatenate([value[:, 640:], digits], axis=1)
        pair_out[s] = jnp.concatenate([value[:, :640], second], axis=0).astype(bf16)
    pl.semaphore_wait(barrier, len(friends))
    pair = [net.send(pair_out.at[s], pair_in.at[s], (part_i, part_t)[s]) for s in range(2)]
    wp[rows(col, 80), :] = w_proj[...]

    streams = ((img, y, y_of, at_i), (txt.at[0], z, z_of, at_t))
    for s in range(2):
        buf, p, of, at = streams[s]
        both[s, pl.ds(pl.multiple_of(at * 24, 8), 24), :] = own[s]
        pair[s].wait_recv()
        other = pair_in[s].astype(f32)
        other = jnp.concatenate([other[:24], other[24:, :512]], axis=1)
        both[s, pl.ds(pl.multiple_of(24 - at * 24, 8), 24), :] = other
        buf[rows(p), :] = both[s].astype(bf16)

    def forward(i):
        r = pl.ds(96 * i, 96)
        states = hid[r, :].astype(f32)
        centered = states - jnp.mean(states, axis=1, keepdims=True)
        rstd = lax.rsqrt(jnp.mean(centered * centered, axis=1, keepdims=True) + eps)
        inner = (centered * rstd * gain[...]).astype(bf16)
        act = nn(inner, w_in[...])
        slope[r, :] = (
            0.5 * (1.0 + lax.erf(act * 0.7071067811865476))
            + act * jnp.exp(-0.5 * act * act) * 0.3989422804014327
        )

    ring = {}
    to_sib = []
    shards = []

    def pass_text(block):
        ref = txt.at[0, rows(block), :]
        to_sib.append(net.send(ref, txt.at[1, rows(block), :], sib))

    for step in range(4):
        for s in range(2):
            buf, p, of, at = streams[s]
            for way in range(2):
                if step:
                    ring[s, way, step - 1].wait_recv()
                origin = lax.rem(p + 8 - step, 8) if way == 0 else lax.rem(p + step, 8)
                cols = slice(0, EX) if step < 3 else (slice(0, 640), slice(640, EX))[way]
                block = buf.at[rows(origin), cols]
                ring[s, way, step] = net.send(block, block, of[1 if way == 0 else 7])
                if s == 1 and (step or way == 0):
                    pass_text(origin)
        if step == 0:
            mine = wp.at[rows(col, 80), :]
            shards += [net.send(mine, mine, x_of[i]) for i in range(1, 4)]
        forward(step)
    for s in range(2):
        for way in range(2):
            ring[s, way, 3].wait_recv()
    pass_text(lax.rem(z + 4, 8))

    edge = (yl == 0) | (yl == 3)
    other_col = lax.rem(col + 8, 16)
    out_dy = jnp.where(yl == 0, -1, 1)
    theirs = wp.at[rows(other_col, 80), :]
    mine = wp.at[rows(col, 80), :]
    seam = net.make(mine, mine, device(x, y + out_dy, z, c))
    inward = pltpu.make_async_remote_copy(
        src_ref=theirs, dst_ref=theirs, send_sem=send_sem.at[N_MSG - 1], recv_sem=seam_recv(net, recv_sem),
        device_id=device(x, y - out_dy, z, c), device_id_type=MESH,
    )

    @pl.when(edge)
    def _():
        seam.start()

    sc[:, 0:384] = logit_scale * nt(img[:, :E], txt[0, :, :E])
    pos[:, 0:384] = jnp.where(nt(img[:, E:], txt[0, :, E:]) > 1.5, 1.0, 0.0)
    for copy in to_sib:
        copy.wait_recv()
    sc[:, 384:768] = logit_scale * nt(img[:, :E], txt[1, :, :E])
    pos[:, 384:768] = jnp.where(nt(img[:, E:], txt[1, :, E:]) > 1.5, 1.0, 0.0)

    first_lane = lax.broadcasted_iota(jnp.int32, (R2, 128), 1) == 0

    def first_pass(i, carry):
        col_peak, col_count = carry
        r = rows(i)
        s, q = sc[r, :], pos[r, :]
        peak = jnp.max(s, axis=1, keepdims=True)
        lse = peak + jnp.log(jnp.sum(jnp.exp(s - peak), axis=1, keepdims=True))
        row_stat[r, :] = jnp.where(first_lane, lse, jnp.sum(q, axis=1, keepdims=True))
        return (
            jnp.maximum(col_peak, jnp.max(s, axis=0, keepdims=True)),
            col_count + jnp.sum(q, axis=0, keepdims=True),
        )

    col_peak, col_count = lax.fori_loop(
        0, 8, first_pass, (jnp.full((1, 768), -1e30, f32), jnp.zeros((1, 768), f32))
    )

    def second_pass(i, total):
        return total + jnp.sum(jnp.exp(sc[rows(i), :] - col_peak), axis=0, keepdims=True)

    col_total = lax.fori_loop(0, 8, second_pass, jnp.zeros((1, 768), f32))
    st_c[0:1, :] = col_peak + jnp.log(col_total)
    st_c[1:2, :] = col_count
    st_r[...] = row_stat[...].T[0:2, :]

    sent = []
    for i in range(1, 8):
        sent.append(net.send(st_c, sl_c.at[z], z_of[i]))
        sent.append(net.send(st_r, sl_r.at[y], y_of[i]))
    sl_c[z] = st_c[...]
    sl_r[y] = st_r[...]

    seam.wait_recv()

    @pl.when(edge)
    def _():
        inward.start()

    for copy in sent:
        copy.wait_recv()
    st_c2[0:1, :] = log_sum_exp([sl_c[i, 0:1, :] for i in range(8)])
    st_c2[1:2, :] = sum(sl_c[i, 1:2, :] for i in range(8))
    st_r2[0:1, :] = log_sum_exp([sl_r[i, 0:1, :] for i in range(8)])
    st_r2[1:2, :] = sum(sl_r[i, 1:2, :] for i in range(8))
    sent = [
        net.send(st_c2, sl_c2.at[0], part_t),
        net.send(st_c2, sl_c2.at[1], sib),
        net.send(st_c2, sl_c2.at[2], part_t_sib),
        net.send(st_r2, sl_r2, part_i),
    ]
    shards += [net.send(theirs, theirs, x_of[i]) for i in range(1, 4)]
    for copy in sent:
        copy.wait_recv()

    def swapped(value):
        return jnp.concatenate([value[:, 384:], value[:, :384]], axis=1)

    quad = [st_c2[...], sl_c2[0], swapped(sl_c2[1]), swapped(sl_c2[2])]
    col_lse = log_sum_exp([v[0:1] for v in quad])
    col_inv = 1.0 / (quad[0][1:2] + quad[1][1:2] + quad[2][1:2] + quad[3][1:2])
    row_lse = log_sum_exp([st_r2[0:1, :], sl_r2[0:1, :]])
    row_inv = 1.0 / (st_r2[1:2, :] + sl_r2[1:2, :])
    row_b[0] = jnp.broadcast_to(row_lse, (128, 384)).T
    row_b[1] = jnp.broadcast_to(row_inv, (128, 384)).T

    def dscore(i, carry):
        r = rows(i)
        s = sc[r, :]
        ds[r, :] = (
            0.5
            * (
                jnp.exp(s - row_b[0, r, 0:1])
                + jnp.exp(s - col_lse)
                - pos[r, :] * (row_b[1, r, 0:1] + col_inv)
            )
        ).astype(bf16)
        return carry

    lax.fori_loop(0, 8, dscore, 0)

    gt[1] = (logit_scale * tn(ds[:, 384:768], img[:, :E])).astype(bf16)
    half = net.send(gt.at[1], gt_sib, sib)
    gt[0] = (logit_scale * tn(ds[:, 0:384], img[:, :E])).astype(bf16)
    gi[...] = (
        logit_scale * (nn(ds[:, 0:384], txt[0, :, :E]) + nn(ds[:, 384:768], txt[1, :, :E]))
    ).astype(bf16)
    half.wait_recv()

    def term(s, block, cols):
        r = rows(block)
        if s == 0:
            return gi[r, cols].astype(f32)
        return gt[0, r, cols].astype(f32) + gt_sib[r, cols].astype(f32)

    halves = (slice(0, 512), slice(512, 1024))
    order = (1, 0)
    for step in range(4):
        for s in order:
            buf, p, of, at = streams[s]
            for way in range(2):
                if step:
                    ring[s, way, "sum", step - 1].wait_recv()
                far = 4 - step
                dest = lax.rem(p + far, 8) if way == 0 else lax.rem(p + 8 - far, 8)
                for h in range(2):
                    if step == 0 and h != way:
                        continue
                    value = term(s, dest, halves[h])
                    if step > 1 or (step == 1 and h == way):
                        value = value + rs_in[s, way, step - 1, :, halves[h]].astype(f32)
                    rs_out[s, way, step, :, halves[h]] = value.astype(bf16)
                cols = halves[way] if step == 0 else slice(0, 1024)
                ring[s, way, "sum", step] = net.send(
                    rs_out.at[s, way, step, :, cols], rs_in.at[s, way, step, :, cols], of[1 if way == 0 else 7]
                )
        if step == 0:
            for copy in shards:
                copy.wait_recv()
            shards = [
                net.send(wp.at[rows(lax.rem(col + 2 * i, 16), 80), :], wp.at[rows(lax.rem(col + 2 * i, 16), 80), :], sib)
                for i in range(8)
            ]
    ends = {}
    for s in order:
        buf, p, of, at = streams[s]
        ring[s, 0, "sum", 3].wait_recv()
        ring[s, 1, "sum", 3].wait_recv()
        for h in halves:
            fin[s, :, h] = term(s, p, h) + rs_in[s, 0, 3, :, h].astype(f32) + rs_in[s, 1, 3, :, h].astype(f32)
        away = fin[s, pl.ds(pl.multiple_of(24 - at * 24, 8), 24), :]
        pr_out[s] = jnp.concatenate([away[:, :512], away[:, 512:]], axis=0).astype(bf16)
        ends[s] = net.send(pr_out.at[s], pr_in.at[s], (part_i, part_t)[s])

    def kept(s):
        ends[s].wait_recv()
        at = streams[s][3]
        mine = fin[s, pl.ds(pl.multiple_of(at * 24, 8), 24), :]
        got = pr_in[s].astype(f32)
        return jnp.concatenate([mine[:, :512] + got[:24], mine[:, 512:] + got[24:]], axis=0)

    slots[col] = kept(1).astype(bf16)
    mine, theirs = slots.at[col], slots.at[other_col]
    over = net.send(mine, mine, y_of[4])
    near = [net.send(mine, mine, x_of[i]) for i in range(1, 4)]
    to_sib = [net.send(mine, mine, sib)]
    final_image = kept(0)
    gi_out[...] = jnp.concatenate([final_image[:24], final_image[24:]], axis=1).astype(bf16)
    over.wait_recv()
    far = [net.send(theirs, theirs, x_of[i]) for i in range(1, 4)]
    to_sib.append(net.send(theirs, theirs, sib))

    def chip_col(half, i):
        return half * 8 + lax.rem(x + i, 4) * 2 + c

    for i in range(1, 4):
        near[i - 1].wait_recv()
        ref = slots.at[chip_col(yh, 4 - i)]
        to_sib.append(net.send(ref, ref, sib))
    for i in range(1, 4):
        far[i - 1].wait_recv()
        ref = slots.at[chip_col(1 - yh, 4 - i)]
        to_sib.append(net.send(ref, ref, sib))
    for copy in to_sib + shards:
        copy.wait_recv()

    def lay(k, carry):
        a, b = slots[2 * k].astype(f32), slots[2 * k + 1].astype(f32)
        gtf[rows(k), 0:512] = jnp.concatenate([a[:24], b[:24]], axis=0).astype(bf16)
        gtf[rows(k), 512:1024] = jnp.concatenate([a[24:], b[24:]], axis=0).astype(bf16)
        return carry

    lax.fori_loop(0, 8, lay, 0)

    dy[...] = nt(gtf[...], wp[...]).astype(bf16)
    dact = (nt(dy[...], w_out[...]) * slope[...]).astype(bf16)
    part[...] = nt(dact, w_in[...]).astype(bf16)
    to_sib = [
        net.send(part.at[rows(2 * i + 1 - c), :], part_sib.at[i], sib) for i in range(4)
    ]
    for copy in to_sib:
        copy.wait_recv()

    def pair_sum(k):
        return part[rows(2 * k + c), :].astype(f32) + part_sib[k].astype(f32)

    near = []
    for i in range(1, 4):
        q_out[i - 1] = pair_sum(lax.rem(x + i, 4)).astype(bf16)
        near.append(net.send(q_out.at[i - 1], q_in.at[i - 1], x_of[i]))
    total = pair_sum(x)
    for i in range(1, 4):
        near[i - 1].wait_recv()
        total = total + q_in[i - 1].astype(f32)
    y_out[...] = total.astype(bf16)
    over = net.send(y_out, y_in, y_of[4])

    my_rows = rows(2 * x + c)
    states = hid[my_rows, :].astype(f32)
    centered = states - jnp.mean(states, axis=1, keepdims=True)
    rstd = lax.rsqrt(jnp.mean(centered * centered, axis=1, keepdims=True) + eps)
    normed = centered * rstd
    over.wait_recv()
    scaled = (y_out[...].astype(f32) + y_in[...].astype(f32)) * gain[...]
    back = rstd * (
        scaled
        - jnp.mean(scaled, axis=1, keepdims=True)
        - normed * jnp.mean(scaled * normed, axis=1, keepdims=True)
    )
    gh_out[my_rows, :] = (dy[my_rows, :].astype(f32) + back).astype(bf16)
    ref = gh_out.at[my_rows, :]
    near = [net.send(ref, ref, x_of[i]) for i in range(1, 4)]
    to_sib = [net.send(ref, ref, sib)]
    for i in range(1, 4):
        near[i - 1].wait_recv()
        ref = gh_out.at[rows(2 * lax.rem(x + 4 - i, 4) + c), :]
        to_sib.append(net.send(ref, ref, sib))
    for copy in to_sib:
        copy.wait_recv()
    net.finish()

    @pl.when(edge)
    def _():
        seam.wait_send()
        inward.wait_send()


def seam_recv(net, recv_sem):
    return recv_sem.at[net.count - 1]


def on_device(image_emb, text_emb, groups, hidden, gain, w_in, w_out, w_proj):
    vmem = pl.BlockSpec(memory_space=pltpu.VMEM)
    scratch = [
        ((2, R2, 640), bf16), ((2, R2, 640), bf16), ((2, R2, EX), f32),
        ((384, EX), bf16), ((2, 384, EX), bf16), ((384, 768), f32), ((384, 768), f32), ((384, 128), f32),
        ((384, 768), bf16), ((384, E), bf16), ((2, 384, E), bf16), ((384, E), bf16),
        ((2, 2, 4, R2, E), bf16), ((2, 2, 4, R2, E), bf16), ((2, R2, E), f32), ((2, R2, 512), bf16), ((2, R2, 512), bf16),
        ((2, 384), f32), ((2, 768), f32), ((8, 2, 384), f32), ((8, 2, 768), f32),
        ((2, 384), f32), ((2, 768), f32), ((2, 384), f32), ((3, 2, 768), f32), ((2, 384, 128), f32),
        ((16, R2, 512), bf16), ((384, E), bf16), ((D, E), bf16), ((384, D), bf16), ((384, FB), f32),
        ((384, D), bf16), ((4, R2, D), bf16), ((3, R2, D), bf16), ((3, R2, D), bf16), ((R2, D), bf16), ((R2, D), bf16),
    ]
    return pl.pallas_call(
        kernel,
        out_shape=(jax.ShapeDtypeStruct((24, E), bf16), jax.ShapeDtypeStruct((384, D), bf16)),
        in_specs=[vmem] * 8,
        out_specs=(vmem, vmem),
        scratch_shapes=[pltpu.VMEM(shape, dtype) for shape, dtype in scratch]
        + [pltpu.SemaphoreType.DMA((N_MSG,)), pltpu.SemaphoreType.DMA((N_MSG,))],
        compiler_params=pltpu.CompilerParams(
            collective_id=0, has_side_effects=True, vmem_limit_bytes=56 * 2**20
        ),
        name="loss_and_block",
    )(image_emb, text_emb, groups.reshape(24, 1), hidden, gain.reshape(1, D), w_in, w_out, w_proj)


def solution(mesh):
    in_specs = (
        P(("row", "col"), None),
        P(("row", "col"), None),
        P(("row", "col")),
        P("row", None),
        P(),
        P(None, "col"),
        P("col", None),
        P("col", None),
    )
    out_specs = (P(("row", "col"), None), P("row", None))
    return jax.shard_map(
        on_device, mesh=mesh, in_specs=in_specs, out_specs=out_specs, check_vma=False
    )
```

```python
import jax
import jax.numpy as jnp
from jax import lax
from jax.experimental import pallas as pl
from jax.experimental.pallas import tpu as pltpu
from jax.sharding import PartitionSpec as P

MESH = pl.DeviceIdType.MESH
bf16, f32 = jnp.bfloat16, jnp.float32
logit_scale = 0.125
eps = 1e-05
E, D, FB = 1024, 1280, 320
EX = E + 128
R2 = 48
N_MSG = 200


def device(x, y, z, c):
    x, y, z = lax.rem(x + 4, 4), lax.rem(y + 8, 8), lax.rem(z + 8, 8)
    return (z * 4 + lax.rem(y, 4), (lax.div(y, 4) * 4 + x) * 2 + c)


def rows(block, size=R2):
    return pl.ds(pl.multiple_of(block * size, 16), size)


class Net:
    def __init__(self, send_sem, recv_sem):
        self.send_sem, self.recv_sem, self.count, self.sent = send_sem, recv_sem, 0, []

    def make(self, src, dst, target):
        copy = pltpu.make_async_remote_copy(
            src_ref=src,
            dst_ref=dst,
            send_sem=self.send_sem.at[self.count],
            recv_sem=self.recv_sem.at[self.count],
            device_id=target,
            device_id_type=MESH,
        )
        self.count += 1
        return copy

    def send(self, src, dst, target):
        copy = self.make(src, dst, target)
        copy.start()
        self.sent.append(copy)
        return copy

    def finish(self):
        for copy in self.sent:
            copy.wait_send()


def nt(a, b):
    return lax.dot_general(a, b, (((1,), (1,)), ((), ())), preferred_element_type=f32)


def tn(a, b):
    return lax.dot_general(a, b, (((0,), (0,)), ((), ())), preferred_element_type=f32)


def nn(a, b):
    return jnp.dot(a, b, preferred_element_type=f32)


def log_sum_exp(parts):
    peak = parts[0]
    for part in parts[1:]:
        peak = jnp.maximum(peak, part)
    total = jnp.exp(parts[0] - peak)
    for part in parts[1:]:
        total = total + jnp.exp(part - peak)
    return peak + jnp.log(total)


def kernel(
    img_in, txt_in, grp, hid_in, gain, w_in_in, w_out_in, w_proj,
    gi_out, gh_out,
    pair_out, pair_in, both,
    img, txt, sc, pos, row_stat, ds, gi, gt, gt_sib,
    rs_out, rs_in, fin, pr_out, pr_in,
    st_r, st_c, sl_r, sl_c, st_r2, st_c2, sl_r2, sl_c2, row_b,
    slots, gtf, wp, dy, slope, part, part_sib, q_out, q_in, y_out, y_in,
    hid, w_in, w_out, send_sem, recv_sem, load_sem,
):
    row, col = lax.axis_index("row"), lax.axis_index("col")
    z, yl = lax.div(row, 4), lax.rem(row, 4)
    yh, c = lax.div(col, 8), lax.rem(col, 2)
    x = lax.rem(lax.div(col, 2), 4)
    y = yh * 4 + yl
    xt = x + 1 - 2 * lax.rem(x, 2)
    xi = 3 - x
    at_t, at_i = lax.rem(x, 2), lax.div(x, 2)
    sib = device(x, y, z, 1 - c)
    part_t, part_i = device(xt, y, z, c), device(xi, y, z, c)
    part_t_sib = device(xt, y, z, 1 - c)
    y_of = [device(x, y + i, z, c) for i in range(8)]
    z_of = [device(x, y, z + i, c) for i in range(8)]
    x_of = [device(x + i, y, z, c) for i in range(4)]
    net = Net(send_sem, recv_sem)

    barrier = pltpu.get_barrier_semaphore()
    friends = y_of[1:] + z_of[1:] + x_of[1:] + [sib, part_t_sib]
    for friend in friends:
        pl.semaphore_signal(barrier, inc=1, device_id=friend, device_id_type=MESH)

    loads = [
        pltpu.make_async_copy(src, dst, load_sem.at[i])
        for i, (src, dst) in enumerate(
            ((w_proj, wp.at[rows(col, 80), :]), (hid_in, hid), (w_in_in, w_in), (w_out_in, w_out))
        )
    ]
    for load in loads:
        load.start()

    lane = lax.broadcasted_iota(jnp.int32, (24, 128), 1)
    line = lax.broadcasted_iota(jnp.int32, (24, 128), 0)
    ids = jnp.full((24, 128), grp[0], jnp.int32)
    for i in range(1, 24):
        ids = jnp.where(line == i, grp[i], ids)
    hit = (lane == lax.shift_right_logical(ids, 6)) | (lane == (ids & 63) + 64)
    digits = jnp.where(hit, 1.0, 0.0).astype(f32)
    own = []
    for s, ref in ((0, img_in), (1, txt_in)):
        value = jnp.concatenate([ref[...].astype(f32), digits], axis=1)
        own.append(value)
        second = jnp.concatenate([value[:, 640:], digits], axis=1)
        pair_out[s] = jnp.concatenate([value[:, :640], second], axis=0).astype(bf16)
    pl.semaphore_wait(barrier, len(friends))
    pair = [net.send(pair_out.at[s], pair_in.at[s], (part_i, part_t)[s]) for s in range(2)]

    streams = ((img, y, y_of, at_i), (txt.at[0], z, z_of, at_t))
    for s in range(2):
        buf, p, of, at = streams[s]
        both[s, pl.ds(pl.multiple_of(at * 24, 8), 24), :] = own[s]
        pair[s].wait_recv()
        other = pair_in[s].astype(f32)
        other = jnp.concatenate([other[:24], other[24:, :512]], axis=1)
        both[s, pl.ds(pl.multiple_of(24 - at * 24, 8), 24), :] = other
        buf[rows(p), :] = both[s].astype(bf16)

    gain_row = gain[...].reshape(1, D)

    def forward(i):
        r = pl.ds(96 * i, 96)
        states = hid[r, :].astype(f32)
        centered = states - jnp.mean(states, axis=1, keepdims=True)
        rstd = lax.rsqrt(jnp.mean(centered * centered, axis=1, keepdims=True) + eps)
        inner = (centered * rstd * gain_row).astype(bf16)
        act = nt(inner, w_in[...])
        slope[r, :] = (
            0.5 * (1.0 + lax.erf(act * 0.7071067811865476))
            + act * jnp.exp(-0.5 * act * act) * 0.3989422804014327
        )

    ring = {}
    to_sib = []
    shards = []

    def pass_text(block):
        ref = txt.at[0, rows(block), :]
        to_sib.append(net.send(ref, txt.at[1, rows(block), :], sib))

    pieces = (slice(0, 640), slice(640, EX))
    for step in range(4):
        for piece in range(2):
            for s in range(2):
                buf, p, of, at = streams[s]
                for way in range(2):
                    if step:
                        ring[s, way, step - 1, piece].wait_recv()
                    origin = lax.rem(p + 8 - step, 8) if way == 0 else lax.rem(p + step, 8)
                    if step < 3 or piece == way:
                        block = buf.at[rows(origin), pieces[piece]]
                        ring[s, way, step, piece] = net.send(block, block, of[1 if way == 0 else 7])
                    if s == 1 and piece == 1 and (step or way == 0):
                        pass_text(origin)
        if step == 0:
            loads[0].wait()
            mine = wp.at[rows(col, 80), :]
            shards += [net.send(mine, mine, x_of[i]) for i in range(1, 4)]
    for s in range(2):
        for way in range(2):
            ring[s, way, 3, way].wait_recv()
    pass_text(lax.rem(z + 4, 8))

    edge = (yl == 0) | (yl == 3)
    other_col = lax.rem(col + 8, 16)
    out_dy = jnp.where(yl == 0, -1, 1)
    theirs = wp.at[rows(other_col, 80), :]
    mine = wp.at[rows(col, 80), :]
    seam = net.make(mine, mine, device(x, y + out_dy, z, c))
    inward = pltpu.make_async_remote_copy(
        src_ref=theirs, dst_ref=theirs, send_sem=send_sem.at[N_MSG - 1], recv_sem=seam_recv(net, recv_sem),
        device_id=device(x, y - out_dy, z, c), device_id_type=MESH,
    )

    @pl.when(edge)
    def _():
        seam.start()

    sc[:, 0:384] = logit_scale * nt(img[:, :E], txt[0, :, :E])
    pos[:, 0:384] = jnp.where(nt(img[:, E:], txt[0, :, E:]) > 1.5, 1.0, 0.0)
    for copy in to_sib:
        copy.wait_recv()
    sc[:, 384:768] = logit_scale * nt(img[:, :E], txt[1, :, :E])
    pos[:, 384:768] = jnp.where(nt(img[:, E:], txt[1, :, E:]) > 1.5, 1.0, 0.0)

    first_lane = lax.broadcasted_iota(jnp.int32, (R2, 128), 1) == 0

    def first_pass(i, carry):
        col_peak, col_count = carry
        r = rows(i)
        s, q = sc[r, :], pos[r, :]
        peak = jnp.max(s, axis=1, keepdims=True)
        lse = peak + jnp.log(jnp.sum(jnp.exp(s - peak), axis=1, keepdims=True))
        row_stat[r, :] = jnp.where(first_lane, lse, jnp.sum(q, axis=1, keepdims=True))
        return (
            jnp.maximum(col_peak, jnp.max(s, axis=0, keepdims=True)),
            col_count + jnp.sum(q, axis=0, keepdims=True),
        )

    col_peak, col_count = lax.fori_loop(
        0, 8, first_pass, (jnp.full((1, 768), -1e30, f32), jnp.zeros((1, 768), f32))
    )

    def second_pass(i, total):
        return total + jnp.sum(jnp.exp(sc[rows(i), :] - col_peak), axis=0, keepdims=True)

    col_total = lax.fori_loop(0, 8, second_pass, jnp.zeros((1, 768), f32))
    st_c[0:1, :] = col_peak + jnp.log(col_total)
    st_c[1:2, :] = col_count
    st_r[...] = row_stat[...].T[0:2, :]

    sent = []
    for i in range(1, 8):
        sent.append(net.send(st_c, sl_c.at[z], z_of[i]))
        sent.append(net.send(st_r, sl_r.at[y], y_of[i]))
    sl_c[z] = st_c[...]
    sl_r[y] = st_r[...]

    seam.wait_recv()

    @pl.when(edge)
    def _():
        inward.start()

    loads[1].wait()
    loads[2].wait()
    forward(0)
    forward(1)
    for copy in sent:
        copy.wait_recv()
    st_c2[0:1, :] = log_sum_exp([sl_c[i, 0:1, :] for i in range(8)])
    st_c2[1:2, :] = sum(sl_c[i, 1:2, :] for i in range(8))
    st_r2[0:1, :] = log_sum_exp([sl_r[i, 0:1, :] for i in range(8)])
    st_r2[1:2, :] = sum(sl_r[i, 1:2, :] for i in range(8))
    sent = [
        net.send(st_c2, sl_c2.at[0], part_t),
        net.send(st_c2, sl_c2.at[1], sib),
        net.send(st_c2, sl_c2.at[2], part_t_sib),
        net.send(st_r2, sl_r2, part_i),
    ]
    shards += [net.send(theirs, theirs, x_of[i]) for i in range(1, 4)]
    forward(2)
    forward(3)
    for copy in sent:
        copy.wait_recv()

    def swapped(value):
        return jnp.concatenate([value[:, 384:], value[:, :384]], axis=1)

    quad = [st_c2[...], sl_c2[0], swapped(sl_c2[1]), swapped(sl_c2[2])]
    col_lse = log_sum_exp([v[0:1] for v in quad])
    col_inv = 1.0 / (quad[0][1:2] + quad[1][1:2] + quad[2][1:2] + quad[3][1:2])
    row_lse = log_sum_exp([st_r2[0:1, :], sl_r2[0:1, :]])
    row_inv = 1.0 / (st_r2[1:2, :] + sl_r2[1:2, :])
    row_b[0] = jnp.broadcast_to(row_lse, (128, 384)).T
    row_b[1] = jnp.broadcast_to(row_inv, (128, 384)).T

    def dscore(i, carry):
        r = rows(i)
        s = sc[r, :]
        ds[r, :] = (
            0.5
            * (
                jnp.exp(s - row_b[0, r, 0:1])
                + jnp.exp(s - col_lse)
                - pos[r, :] * (row_b[1, r, 0:1] + col_inv)
            )
        ).astype(bf16)
        return carry

    lax.fori_loop(0, 8, dscore, 0)

    gt[1] = (logit_scale * tn(ds[:, 384:768], img[:, :E])).astype(bf16)
    half = net.send(gt.at[1], gt_sib, sib)
    gt[0] = (logit_scale * tn(ds[:, 0:384], img[:, :E])).astype(bf16)
    gi[...] = (
        logit_scale * (nn(ds[:, 0:384], txt[0, :, :E]) + nn(ds[:, 384:768], txt[1, :, :E]))
    ).astype(bf16)
    half.wait_recv()

    def term(s, block, cols):
        r = rows(block)
        if s == 0:
            return gi[r, cols].astype(f32)
        return gt[0, r, cols].astype(f32) + gt_sib[r, cols].astype(f32)

    halves = (slice(0, 512), slice(512, 1024))
    order = (1, 0)
    for step in range(4):
        for h in range(2):
            for s in order:
                buf, p, of, at = streams[s]
                for way in range(2):
                    if step == 0 and h != way:
                        continue
                    far = 4 - step
                    dest = lax.rem(p + far, 8) if way == 0 else lax.rem(p + 8 - far, 8)
                    value = term(s, dest, halves[h])
                    if step > 1 or (step == 1 and h == way):
                        ring[s, way, "sum", step - 1, h].wait_recv()
                        value = value + rs_in[s, way, step - 1, :, halves[h]].astype(f32)
                    rs_out[s, way, step, :, halves[h]] = value.astype(bf16)
                    ring[s, way, "sum", step, h] = net.send(
                        rs_out.at[s, way, step, :, halves[h]],
                        rs_in.at[s, way, step, :, halves[h]],
                        of[1 if way == 0 else 7],
                    )
        if step == 2:
            for copy in shards:
                copy.wait_recv()
            shards = []
            for i in range(8):
                ref = wp.at[rows(lax.rem(col + 2 * i, 16), 80), :]
                shards.append(net.send(ref, ref, sib))
    ends = {}
    for s in order:
        buf, p, of, at = streams[s]
        for i, h in enumerate(halves):
            ring[s, 0, "sum", 3, i].wait_recv()
            ring[s, 1, "sum", 3, i].wait_recv()
            fin[s, :, h] = term(s, p, h) + rs_in[s, 0, 3, :, h].astype(f32) + rs_in[s, 1, 3, :, h].astype(f32)
        away = fin[s, pl.ds(pl.multiple_of(24 - at * 24, 8), 24), :]
        pr_out[s] = jnp.concatenate([away[:, :512], away[:, 512:]], axis=0).astype(bf16)
        ends[s] = net.send(pr_out.at[s], pr_in.at[s], (part_i, part_t)[s])

    def kept(s):
        ends[s].wait_recv()
        at = streams[s][3]
        mine = fin[s, pl.ds(pl.multiple_of(at * 24, 8), 24), :]
        got = pr_in[s].astype(f32)
        return jnp.concatenate([mine[:, :512] + got[:24], mine[:, 512:] + got[24:]], axis=0)

    slots[col] = kept(1).astype(bf16)
    mine, theirs = slots.at[col], slots.at[other_col]
    over = net.send(mine, mine, y_of[4])
    near = [net.send(mine, mine, x_of[i]) for i in range(1, 4)]
    to_sib = [net.send(mine, mine, sib)]
    final_image = kept(0)
    gi_out[...] = jnp.concatenate([final_image[:24], final_image[24:]], axis=1).astype(bf16)
    over.wait_recv()
    far = [net.send(theirs, theirs, x_of[i]) for i in range(1, 4)]
    to_sib.append(net.send(theirs, theirs, sib))

    def chip_col(half, i):
        return half * 8 + lax.rem(x + i, 4) * 2 + c

    def lay(k, carry):
        a, b = slots[2 * k].astype(f32), slots[2 * k + 1].astype(f32)
        gtf[rows(k), 0:512] = jnp.concatenate([a[:24], b[:24]], axis=0).astype(bf16)
        gtf[rows(k), 512:1024] = jnp.concatenate([a[24:], b[24:]], axis=0).astype(bf16)
        return carry

    def block_backward(half):
        lax.fori_loop(half * 4, half * 4 + 4, lay, 0)
        r = rows(half, 192)
        dy[r, :] = nt(gtf[r, :], wp[...]).astype(bf16)
        dact = (nt(dy[r, :], w_out[...]) * slope[r, :]).astype(bf16)
        part[r, :] = nn(dact, w_in[...]).astype(bf16)

    for i in range(1, 4):
        near[i - 1].wait_recv()
        ref = slots.at[chip_col(yh, 4 - i)]
        to_sib.append(net.send(ref, ref, sib))
    for i in range(1, 4):
        far[i - 1].wait_recv()
        ref = slots.at[chip_col(1 - yh, 4 - i)]
        to_sib.append(net.send(ref, ref, sib))
    loads[3].wait()
    near_sib, far_sib = [to_sib[i] for i in (0, 2, 3, 4)], [to_sib[i] for i in (1, 5, 6, 7)]
    for copy in near_sib + shards:
        copy.wait_recv()
    block_backward(yh)

    def piece(block, t):
        return pl.ds(pl.multiple_of(block * R2 + 16 * t, 16), 16)

    early = []
    for i in range(2):
        k = 2 * yh + i
        early.append(net.send(part.at[rows(2 * k + 1 - c), :], part_sib.at[k], sib))
    for copy in far_sib:
        copy.wait_recv()
    block_backward(1 - yh)
    late = {}
    for t in range(3):
        for i in range(2):
            k = 2 * (1 - yh) + i
            late[t, i] = net.send(part.at[piece(2 * k + 1 - c, t), :], part_sib.at[k, pl.ds(16 * t, 16)], sib)
    for copy in early:
        copy.wait_recv()

    def pair_sum(k, t):
        return part[piece(2 * k + c, t), :].astype(f32) + part_sib[k, pl.ds(16 * t, 16), :].astype(f32)

    steps = [pl.ds(16 * t, 16) for t in range(3)]
    around = {}
    for t, r in enumerate(steps):
        late[t, 0].wait_recv()
        late[t, 1].wait_recv()
        for i in (2, 1, 3):
            q_out[i - 1, r, :] = pair_sum(lax.rem(x + i, 4), t).astype(bf16)
            around[t, i] = net.send(q_out.at[i - 1, r], q_in.at[i - 1, r], x_of[i])
    over = []
    for t, r in enumerate(steps):
        total = pair_sum(x, t)
        for i in (1, 3, 2):
            around[t, i].wait_recv()
            total = total + q_in[i - 1, r, :].astype(f32)
        y_out[r, :] = total.astype(bf16)
        over.append(net.send(y_out.at[r], y_in.at[r], y_of[4]))

    to_sib = []
    for t, r in enumerate(steps):
        mine = piece(2 * x + c, t)
        states = hid[mine, :].astype(f32)
        centered = states - jnp.mean(states, axis=1, keepdims=True)
        rstd = lax.rsqrt(jnp.mean(centered * centered, axis=1, keepdims=True) + eps)
        normed = centered * rstd
        over[t].wait_recv()
        scaled = (y_out[r, :].astype(f32) + y_in[r, :].astype(f32)) * gain_row
        back = rstd * (
            scaled
            - jnp.mean(scaled, axis=1, keepdims=True)
            - normed * jnp.mean(scaled * normed, axis=1, keepdims=True)
        )
        gh_out[mine, :] = (dy[mine, :].astype(f32) + back).astype(bf16)
        ref = gh_out.at[mine, :]
        for i in (2, 1, 3):
            around[t, i] = net.send(ref, ref, x_of[i])
        to_sib.append(net.send(ref, ref, sib))
    for t in range(3):
        for i in (1, 3, 2):
            around[t, i].wait_recv()
            ref = gh_out.at[piece(2 * lax.rem(x + 4 - i, 4) + c, t), :]
            to_sib.append(net.send(ref, ref, sib))
    for copy in to_sib:
        copy.wait_recv()
    net.finish()

    @pl.when(edge)
    def _():
        seam.wait_send()
        inward.wait_send()


def seam_recv(net, recv_sem):
    return recv_sem.at[net.count - 1]


def hand_over(gi, gh, gi_out, gh_out, held, in_sem, out_sem):
    pieces = [pl.ds(96 * i, 96) for i in range(4)]
    reads = [pltpu.make_async_copy(gh.at[p], held.at[p], in_sem.at[i]) for i, p in enumerate(pieces)]
    writes = [pltpu.make_async_copy(held.at[p], gh_out.at[p], out_sem.at[i]) for i, p in enumerate(pieces)]
    for copy in reads:
        copy.start()
    gi_out[...] = gi[...]
    for read, write in zip(reads, writes):
        read.wait()
        write.start()
    for copy in writes:
        copy.wait()


def on_device(image_emb, text_emb, groups, hidden, gain, w_in, w_out, w_proj):
    vmem = pl.BlockSpec(memory_space=pltpu.VMEM)
    shapes = (jax.ShapeDtypeStruct((24, E), bf16), jax.ShapeDtypeStruct((384, D), bf16))
    scratch = [
        ((2, R2, 640), bf16), ((2, R2, 640), bf16), ((2, R2, EX), f32),
        ((384, EX), bf16), ((2, 384, EX), bf16), ((384, 768), f32), ((384, 768), f32), ((384, 128), f32),
        ((384, 768), bf16), ((384, E), bf16), ((2, 384, E), bf16), ((384, E), bf16),
        ((2, 2, 4, R2, E), bf16), ((2, 2, 4, R2, E), bf16), ((2, R2, E), f32), ((2, R2, 512), bf16), ((2, R2, 512), bf16),
        ((2, 384), f32), ((2, 768), f32), ((8, 2, 384), f32), ((8, 2, 768), f32),
        ((2, 384), f32), ((2, 768), f32), ((2, 384), f32), ((3, 2, 768), f32), ((2, 384, 128), f32),
        ((16, R2, 512), bf16), ((384, E), bf16), ((D, E), bf16), ((384, D), bf16), ((384, FB), f32),
        ((384, D), bf16), ((4, R2, D), bf16), ((3, R2, D), bf16), ((3, R2, D), bf16), ((R2, D), bf16), ((R2, D), bf16),
        ((384, D), bf16), ((FB, D), bf16), ((FB, D), bf16),
    ]
    anywhere = pl.BlockSpec(memory_space=pl.ANY)
    results = pl.pallas_call(
        kernel,
        out_shape=shapes,
        in_specs=[vmem, vmem, pl.BlockSpec(memory_space=pltpu.SMEM), anywhere, vmem] + [anywhere] * 3,
        out_specs=(vmem, vmem),
        scratch_shapes=[pltpu.VMEM(shape, dtype) for shape, dtype in scratch]
        + [pltpu.SemaphoreType.DMA((N_MSG,)), pltpu.SemaphoreType.DMA((N_MSG,)), pltpu.SemaphoreType.DMA((4,))],
        compiler_params=pltpu.CompilerParams(
            collective_id=0, has_side_effects=True, vmem_limit_bytes=56 * 2**20
        ),
        name="loss_and_block",
    )(image_emb, text_emb, groups, hidden, gain, w_in.T, w_out, w_proj)
    return pl.pallas_call(
        hand_over,
        out_shape=shapes,
        in_specs=[vmem, anywhere],
        out_specs=(vmem, anywhere),
        scratch_shapes=[pltpu.VMEM((384, D), bf16), pltpu.SemaphoreType.DMA((4,)), pltpu.SemaphoreType.DMA((4,))],
        compiler_params=pltpu.CompilerParams(vmem_limit_bytes=56 * 2**20),
        name="hand_over",
    )(*results)


def solution(mesh):
    in_specs = (
        P(("row", "col"), None),
        P(("row", "col"), None),
        P(("row", "col")),
        P("row", None),
        P(),
        P(None, "col"),
        P("col", None),
        P("col", None),
    )
    out_specs = (P(("row", "col"), None), P("row", None))
    return jax.shard_map(
        on_device, mesh=mesh, in_specs=in_specs, out_specs=out_specs, check_vma=False
    )
```

```python
import jax
import jax.numpy as jnp
from jax import lax
from jax.experimental import pallas as pl
from jax.experimental.pallas import tpu as pltpu
from jax.sharding import PartitionSpec as P

MESH = pl.DeviceIdType.MESH
bf16, f32 = jnp.bfloat16, jnp.float32
logit_scale = 0.125
eps = 1e-05
E, D, FB = 1024, 1280, 320
EX = E + 128
R2 = 48
N_MSG = 200


def device(x, y, z, c):
    x, y, z = lax.rem(x + 4, 4), lax.rem(y + 8, 8), lax.rem(z + 8, 8)
    return (z * 4 + lax.rem(y, 4), (lax.div(y, 4) * 4 + x) * 2 + c)


def rows(block, size=R2):
    return pl.ds(pl.multiple_of(block * size, 16), size)


class Net:
    def __init__(self, send_sem, recv_sem):
        self.send_sem, self.recv_sem, self.count, self.sent = send_sem, recv_sem, 0, []

    def make(self, src, dst, target):
        copy = pltpu.make_async_remote_copy(
            src_ref=src,
            dst_ref=dst,
            send_sem=self.send_sem.at[self.count],
            recv_sem=self.recv_sem.at[self.count],
            device_id=target,
            device_id_type=MESH,
        )
        self.count += 1
        return copy

    def send(self, src, dst, target):
        copy = self.make(src, dst, target)
        copy.start()
        self.sent.append(copy)
        return copy

    def finish(self):
        for copy in self.sent:
            copy.wait_send()


def nt(a, b):
    return lax.dot_general(a, b, (((1,), (1,)), ((), ())), preferred_element_type=f32)


def tn(a, b):
    return lax.dot_general(a, b, (((0,), (0,)), ((), ())), preferred_element_type=f32)


def nn(a, b):
    return jnp.dot(a, b, preferred_element_type=f32)


def log_sum_exp(parts):
    peak = parts[0]
    for part in parts[1:]:
        peak = jnp.maximum(peak, part)
    total = jnp.exp(parts[0] - peak)
    for part in parts[1:]:
        total = total + jnp.exp(part - peak)
    return peak + jnp.log(total)


def kernel(
    img_in, txt_in, grp, hid_in, gain, w_in_in, w_out_in, w_proj,
    gi_out, gh_out,
    pair_out, pair_in, both,
    img, txt, sc, pos, row_stat, ds, gi, gt, gt_sib,
    rs_out, rs_in, fin, pr_out, pr_in,
    st_r, st_c, sl_r, sl_c, st_r2, st_c2, sl_r2, sl_c2, row_b,
    slots, gtf, wp, dy, slope, part, q_in, y_out, y_in,
    hid, hid_own, wide, w_in, w_out, send_sem, recv_sem, load_sem,
):
    row, col = lax.axis_index("row"), lax.axis_index("col")
    z, yl = lax.div(row, 4), lax.rem(row, 4)
    yh, c = lax.div(col, 8), lax.rem(col, 2)
    x = lax.rem(lax.div(col, 2), 4)
    y = yh * 4 + yl
    xt = x + 1 - 2 * lax.rem(x, 2)
    xi = 3 - x
    at_t, at_i = lax.rem(x, 2), lax.div(x, 2)
    sib = device(x, y, z, 1 - c)
    part_t, part_i = device(xt, y, z, c), device(xi, y, z, c)
    part_t_sib = device(xt, y, z, 1 - c)
    y_of = [device(x, y + i, z, c) for i in range(8)]
    z_of = [device(x, y, z + i, c) for i in range(8)]
    x_of = [device(x + i, y, z, c) for i in range(4)]
    net = Net(send_sem, recv_sem)

    barrier = pltpu.get_barrier_semaphore()
    friends = y_of[1:] + z_of[1:] + x_of[1:] + [sib, part_t_sib]
    for friend in friends:
        pl.semaphore_signal(barrier, inc=1, device_id=friend, device_id_type=MESH)

    loads = [
        pltpu.make_async_copy(src, dst, load_sem.at[i])
        for i, (src, dst) in enumerate(
            ((w_proj, wp.at[rows(col, 80), :]), (hid_in, hid), (w_in_in, w_in.at[0]), (w_out_in, w_out.at[0]))
        )
    ]
    for load in loads:
        load.start()

    lane = lax.broadcasted_iota(jnp.int32, (24, 128), 1)
    line = lax.broadcasted_iota(jnp.int32, (24, 128), 0)
    ids = jnp.full((24, 128), grp[0], jnp.int32)
    for i in range(1, 24):
        ids = jnp.where(line == i, grp[i], ids)
    hit = (lane == lax.shift_right_logical(ids, 6)) | (lane == (ids & 63) + 64)
    digits = jnp.where(hit, 1.0, 0.0).astype(f32)
    own = []
    for s, ref in ((0, img_in), (1, txt_in)):
        value = jnp.concatenate([ref[...].astype(f32), digits], axis=1)
        own.append(value)
        second = jnp.concatenate([value[:, 640:], digits], axis=1)
        pair_out[s] = jnp.concatenate([value[:, :640], second], axis=0).astype(bf16)
    pl.semaphore_wait(barrier, len(friends))
    pair = [net.send(pair_out.at[s], pair_in.at[s], (part_i, part_t)[s]) for s in range(2)]

    streams = ((img, y, y_of, at_i), (txt.at[0], z, z_of, at_t))
    for s in range(2):
        buf, p, of, at = streams[s]
        both[s, pl.ds(pl.multiple_of(at * 24, 8), 24), :] = own[s]
        pair[s].wait_recv()
        other = pair_in[s].astype(f32)
        other = jnp.concatenate([other[:24], other[24:, :512]], axis=1)
        both[s, pl.ds(pl.multiple_of(24 - at * 24, 8), 24), :] = other
        buf[rows(p), :] = both[s].astype(bf16)

    gain_row = gain[...].reshape(1, D)

    def forward(i):
        halves = []
        for k in range(2):
            wide[k] = hid[pl.ds(96 * i + R2 * k, R2), :].astype(f32)
            halves.append(wide[k, pl.ds(pl.multiple_of(24 * c, 8), 24), :])
        states = jnp.concatenate(halves, axis=0)
        r = pl.ds(R2 * i, R2)
        hid_own[r, :] = states.astype(bf16)
        centered = states - jnp.mean(states, axis=1, keepdims=True)
        rstd = lax.rsqrt(jnp.mean(centered * centered, axis=1, keepdims=True) + eps)
        inner = (centered * rstd * gain_row).astype(bf16)
        for k in range(2):
            act = nt(inner, w_in[k])
            slope[k, r, :] = (
                0.5 * (1.0 + lax.erf(act * 0.7071067811865476))
                + act * jnp.exp(-0.5 * act * act) * 0.3989422804014327
            )

    ring = {}
    to_sib = []
    shards = []

    def pass_text(block):
        ref = txt.at[0, rows(block), :]
        to_sib.append(net.send(ref, txt.at[1, rows(block), :], sib))

    pieces = (slice(0, 640), slice(640, EX))
    for step in range(4):
        for piece in range(2):
            for s in range(2):
                buf, p, of, at = streams[s]
                for way in range(2):
                    if step:
                        ring[s, way, step - 1, piece].wait_recv()
                    origin = lax.rem(p + 8 - step, 8) if way == 0 else lax.rem(p + step, 8)
                    if step < 3 or piece == way:
                        block = buf.at[rows(origin), pieces[piece]]
                        ring[s, way, step, piece] = net.send(block, block, of[1 if way == 0 else 7])
                    if s == 1 and piece == 1 and (step or way == 0):
                        pass_text(origin)
        if step == 0:
            loads[0].wait()
            mine = wp.at[rows(col, 80), :]
            shards += [net.send(mine, mine, x_of[i]) for i in range(1, 4)]
            loads[2].wait()
            loads[3].wait()
            weights = [net.send(w_in.at[0], w_in.at[1], sib), net.send(w_out.at[0], w_out.at[1], sib)]
    for s in range(2):
        for way in range(2):
            ring[s, way, 3, way].wait_recv()
    pass_text(lax.rem(z + 4, 8))

    edge = (yl == 0) | (yl == 3)
    other_col = lax.rem(col + 8, 16)
    out_dy = jnp.where(yl == 0, -1, 1)
    theirs = wp.at[rows(other_col, 80), :]
    mine = wp.at[rows(col, 80), :]
    seam = net.make(mine, mine, device(x, y + out_dy, z, c))
    inward = pltpu.make_async_remote_copy(
        src_ref=theirs, dst_ref=theirs, send_sem=send_sem.at[N_MSG - 1], recv_sem=seam_recv(net, recv_sem),
        device_id=device(x, y - out_dy, z, c), device_id_type=MESH,
    )

    @pl.when(edge)
    def _():
        seam.start()

    sc[:, 0:384] = logit_scale * nt(img[:, :E], txt[0, :, :E])
    pos[:, 0:384] = jnp.where(nt(img[:, E:], txt[0, :, E:]) > 1.5, 1.0, 0.0)
    for copy in to_sib:
        copy.wait_recv()
    sc[:, 384:768] = logit_scale * nt(img[:, :E], txt[1, :, :E])
    pos[:, 384:768] = jnp.where(nt(img[:, E:], txt[1, :, E:]) > 1.5, 1.0, 0.0)

    first_lane = lax.broadcasted_iota(jnp.int32, (R2, 128), 1) == 0

    def first_pass(i, carry):
        col_peak, col_count = carry
        r = rows(i)
        s, q = sc[r, :], pos[r, :]
        peak = jnp.max(s, axis=1, keepdims=True)
        lse = peak + jnp.log(jnp.sum(jnp.exp(s - peak), axis=1, keepdims=True))
        row_stat[r, :] = jnp.where(first_lane, lse, jnp.sum(q, axis=1, keepdims=True))
        return (
            jnp.maximum(col_peak, jnp.max(s, axis=0, keepdims=True)),
            col_count + jnp.sum(q, axis=0, keepdims=True),
        )

    col_peak, col_count = lax.fori_loop(
        0, 8, first_pass, (jnp.full((1, 768), -1e30, f32), jnp.zeros((1, 768), f32))
    )

    def second_pass(i, total):
        return total + jnp.sum(jnp.exp(sc[rows(i), :] - col_peak), axis=0, keepdims=True)

    col_total = lax.fori_loop(0, 8, second_pass, jnp.zeros((1, 768), f32))
    st_c[0:1, :] = col_peak + jnp.log(col_total)
    st_c[1:2, :] = col_count
    st_r[...] = row_stat[...].T[0:2, :]

    sent = []
    for i in range(1, 8):
        sent.append(net.send(st_c, sl_c.at[z], z_of[i]))
        sent.append(net.send(st_r, sl_r.at[y], y_of[i]))
    sl_c[z] = st_c[...]
    sl_r[y] = st_r[...]

    seam.wait_recv()

    @pl.when(edge)
    def _():
        inward.start()

    loads[1].wait()
    weights[0].wait_recv()
    forward(0)
    forward(1)
    for copy in sent:
        copy.wait_recv()
    st_c2[0:1, :] = log_sum_exp([sl_c[i, 0:1, :] for i in range(8)])
    st_c2[1:2, :] = sum(sl_c[i, 1:2, :] for i in range(8))
    st_r2[0:1, :] = log_sum_exp([sl_r[i, 0:1, :] for i in range(8)])
    st_r2[1:2, :] = sum(sl_r[i, 1:2, :] for i in range(8))
    sent = [
        net.send(st_c2, sl_c2.at[0], part_t),
        net.send(st_c2, sl_c2.at[1], sib),
        net.send(st_c2, sl_c2.at[2], part_t_sib),
        net.send(st_r2, sl_r2, part_i),
    ]
    shards += [net.send(theirs, theirs, x_of[i]) for i in range(1, 4)]
    forward(2)
    forward(3)
    for copy in sent:
        copy.wait_recv()

    def swapped(value):
        return jnp.concatenate([value[:, 384:], value[:, :384]], axis=1)

    quad = [st_c2[...], sl_c2[0], swapped(sl_c2[1]), swapped(sl_c2[2])]
    col_lse = log_sum_exp([v[0:1] for v in quad])
    col_inv = 1.0 / (quad[0][1:2] + quad[1][1:2] + quad[2][1:2] + quad[3][1:2])
    row_lse = log_sum_exp([st_r2[0:1, :], sl_r2[0:1, :]])
    row_inv = 1.0 / (st_r2[1:2, :] + sl_r2[1:2, :])
    row_b[0] = jnp.broadcast_to(row_lse, (128, 384)).T
    row_b[1] = jnp.broadcast_to(row_inv, (128, 384)).T

    def dscore(i, carry):
        r = rows(i)
        s = sc[r, :]
        ds[r, :] = (
            0.5
            * (
                jnp.exp(s - row_b[0, r, 0:1])
                + jnp.exp(s - col_lse)
                - pos[r, :] * (row_b[1, r, 0:1] + col_inv)
            )
        ).astype(bf16)
        return carry

    lax.fori_loop(0, 8, dscore, 0)

    gi[...] = (
        logit_scale * (nn(ds[:, 0:384], txt[0, :, :E]) + nn(ds[:, 384:768], txt[1, :, :E]))
    ).astype(bf16)

    def term(s, block, cols):
        r = rows(block)
        if s == 0:
            return gi[r, cols].astype(f32)
        return gt[0, r, cols].astype(f32) + gt_sib[r, cols].astype(f32)

    halves = (slice(0, 512), slice(512, 1024))

    def ring_step(s, step):
        buf, p, of, at = streams[s]
        for h in range(2):
            for way in range(2):
                if step == 0 and h != way:
                    continue
                far = 4 - step
                dest = lax.rem(p + far, 8) if way == 0 else lax.rem(p + 8 - far, 8)
                value = term(s, dest, halves[h])
                if step > 1 or (step == 1 and h == way):
                    ring[s, way, "sum", step - 1, h].wait_recv()
                    value = value + rs_in[s, way, step - 1, :, halves[h]].astype(f32)
                rs_out[s, way, step, :, halves[h]] = value.astype(bf16)
                ring[s, way, "sum", step, h] = net.send(
                    rs_out.at[s, way, step, :, halves[h]],
                    rs_in.at[s, way, step, :, halves[h]],
                    of[1 if way == 0 else 7],
                )

    ends = {}

    def ring_end(s):
        buf, p, of, at = streams[s]
        for i, h in enumerate(halves):
            ring[s, 0, "sum", 3, i].wait_recv()
            ring[s, 1, "sum", 3, i].wait_recv()
            fin[s, :, h] = term(s, p, h) + rs_in[s, 0, 3, :, h].astype(f32) + rs_in[s, 1, 3, :, h].astype(f32)
        away = fin[s, pl.ds(pl.multiple_of(24 - at * 24, 8), 24), :]
        pr_out[s] = jnp.concatenate([away[:, :512], away[:, 512:]], axis=0).astype(bf16)
        ends[s] = net.send(pr_out.at[s], pr_in.at[s], (part_i, part_t)[s])

    def kept(s):
        ends[s].wait_recv()
        at = streams[s][3]
        mine = fin[s, pl.ds(pl.multiple_of(at * 24, 8), 24), :]
        got = pr_in[s].astype(f32)
        return jnp.concatenate([mine[:, :512] + got[:24], mine[:, 512:] + got[24:]], axis=0)

    ring_step(0, 0)
    gt[1] = (logit_scale * tn(ds[:, 384:768], img[:, :E])).astype(bf16)
    half = net.send(gt.at[1], gt_sib, sib)
    gt[0] = (logit_scale * tn(ds[:, 0:384], img[:, :E])).astype(bf16)
    ring_step(0, 1)
    half.wait_recv()
    ring_step(1, 0)
    ring_step(0, 2)
    for copy in shards:
        copy.wait_recv()
    shards = []
    for i in range(8):
        ref = wp.at[rows(lax.rem(col + 2 * i, 16), 80), :]
        shards.append(net.send(ref, ref, sib))
    ring_step(1, 1)
    ring_step(0, 3)
    ring_step(1, 2)
    ring_end(0)
    ring_step(1, 3)

    chip = yh * 4 + x
    slots[chip] = kept(0).astype(bf16)
    mine, theirs = slots.at[chip], slots.at[lax.rem(chip + 4, 8)]
    over = net.send(mine, mine, y_of[4])
    near = {i: net.send(mine, mine, x_of[i]) for i in (2, 1, 3)}
    ring_end(1)
    over.wait_recv()
    far = {i: net.send(theirs, theirs, x_of[i]) for i in (2, 1, 3)}

    def lay(k, carry):
        a, b = slots[2 * k].astype(f32), slots[2 * k + 1].astype(f32)
        gtf[rows(k), 0:512] = jnp.concatenate([a[:24], b[:24]], axis=0).astype(bf16)
        gtf[rows(k), 512:1024] = jnp.concatenate([a[24:], b[24:]], axis=0).astype(bf16)
        return carry

    def block_backward(half):
        lax.fori_loop(half * 2, half * 2 + 2, lay, 0)
        r = rows(half, 96)
        dy[r, :] = nt(gtf[r, :], wp[...]).astype(bf16)
        dinner = 0.0
        for k in range(2):
            dact = (nt(dy[r, :], w_out[k]) * slope[k, r, :]).astype(bf16)
            dinner = dinner + nn(dact, w_in[k])
        part[r, :] = dinner.astype(bf16)

    weights[1].wait_recv()
    for copy in shards + list(near.values()):
        copy.wait_recv()
    block_backward(yh)
    for copy in far.values():
        copy.wait_recv()
    block_backward(1 - yh)

    def piece(block, t):
        return pl.ds(pl.multiple_of(block * R2 + 16 * t, 16), 16)

    steps = [pl.ds(16 * t, 16) for t in range(3)]
    around = {}
    for t, r in enumerate(steps):
        for i in (2, 1, 3):
            around[t, i] = net.send(part.at[piece(lax.rem(x + i, 4), t), :], q_in.at[i - 1, r], x_of[i])
    final_image = kept(1)
    gi_out[...] = jnp.concatenate([final_image[:24], final_image[24:]], axis=1).astype(bf16)
    over = []
    for t, r in enumerate(steps):
        total = part[piece(x, t), :].astype(f32)
        for i in (1, 3, 2):
            around[t, i].wait_recv()
            total = total + q_in[i - 1, r, :].astype(f32)
        y_out[r, :] = total.astype(bf16)
        over.append(net.send(y_out.at[r], y_in.at[r], y_of[4]))

    to_sib = []
    for t, r in enumerate(steps):
        mine = piece(x, t)
        states = hid_own[mine, :].astype(f32)
        centered = states - jnp.mean(states, axis=1, keepdims=True)
        rstd = lax.rsqrt(jnp.mean(centered * centered, axis=1, keepdims=True) + eps)
        normed = centered * rstd
        over[t].wait_recv()
        scaled = (y_out[r, :].astype(f32) + y_in[r, :].astype(f32)) * gain_row
        back = rstd * (
            scaled
            - jnp.mean(scaled, axis=1, keepdims=True)
            - normed * jnp.mean(scaled * normed, axis=1, keepdims=True)
        )
        gh_out[c, mine, :] = (dy[mine, :].astype(f32) + back).astype(bf16)
        ref = gh_out.at[c, mine, :]
        for i in (2, 1, 3):
            around[t, i] = net.send(ref, ref, x_of[i])
        to_sib.append(net.send(ref, ref, sib))
    for t in range(3):
        for i in (1, 3, 2):
            around[t, i].wait_recv()
            ref = gh_out.at[c, piece(lax.rem(x + 4 - i, 4), t), :]
            to_sib.append(net.send(ref, ref, sib))
    for copy in to_sib:
        copy.wait_recv()
    net.finish()

    @pl.when(edge)
    def _():
        seam.wait_send()
        inward.wait_send()


def seam_recv(net, recv_sem):
    return recv_sem.at[net.count - 1]


def hand_over(gi, gh, gi_out, gh_out, gi_held, held, laid, sem):
    pieces = [pl.ds(R2 * i, R2) for i in range(4)]
    reads = [pltpu.make_async_copy(gh.at[:, p], held.at[:, p], sem.at[i]) for i, p in enumerate(pieces)]
    first = pltpu.make_async_copy(gi, gi_held, sem.at[4])
    last = pltpu.make_async_copy(gi_held, gi_out, sem.at[5])
    first.start()
    for copy in reads:
        copy.start()
    first.wait()
    last.start()
    writes = []
    for i, p in enumerate(pieces):
        reads[i].wait()
        a, b = held[0, p, :].astype(f32), held[1, p, :].astype(f32)
        out = pl.ds(96 * i, 96)
        laid[out, :] = jnp.concatenate([a[:24], b[:24], a[24:], b[24:]], axis=0).astype(bf16)
        writes.append(pltpu.make_async_copy(laid.at[out], gh_out.at[out], sem.at[6 + i]))
        writes[i].start()
    for copy in writes + [last]:
        copy.wait()


def on_device(image_emb, text_emb, groups, hidden, gain, w_in, w_out, w_proj):
    vmem = pl.BlockSpec(memory_space=pltpu.VMEM)
    shapes = (jax.ShapeDtypeStruct((24, E), bf16), jax.ShapeDtypeStruct((384, D), bf16))
    scratch = [
        ((2, R2, 640), bf16), ((2, R2, 640), bf16), ((2, R2, EX), f32),
        ((384, EX), bf16), ((2, 384, EX), bf16), ((384, 768), f32), ((384, 768), f32), ((384, 128), f32),
        ((384, 768), bf16), ((384, E), bf16), ((2, 384, E), bf16), ((384, E), bf16),
        ((2, 2, 4, R2, E), bf16), ((2, 2, 4, R2, E), bf16), ((2, R2, E), f32), ((2, R2, 512), bf16), ((2, R2, 512), bf16),
        ((2, 384), f32), ((2, 768), f32), ((8, 2, 384), f32), ((8, 2, 768), f32),
        ((2, 384), f32), ((2, 768), f32), ((2, 384), f32), ((3, 2, 768), f32), ((2, 384, 128), f32),
        ((8, R2, 512), bf16), ((192, E), bf16), ((D, E), bf16), ((192, D), bf16), ((2, 192, FB), f32),
        ((192, D), bf16), ((3, R2, D), bf16), ((R2, D), bf16), ((R2, D), bf16),
        ((384, D), bf16), ((192, D), bf16), ((2, R2, D), f32), ((2, FB, D), bf16), ((2, FB, D), bf16),
    ]
    anywhere = pl.BlockSpec(memory_space=pl.ANY)
    results = pl.pallas_call(
        kernel,
        out_shape=(shapes[0], jax.ShapeDtypeStruct((2, 192, D), bf16)),
        in_specs=[vmem, vmem, pl.BlockSpec(memory_space=pltpu.SMEM), anywhere, vmem] + [anywhere] * 3,
        out_specs=(vmem, vmem),
        scratch_shapes=[pltpu.VMEM(shape, dtype) for shape, dtype in scratch]
        + [pltpu.SemaphoreType.DMA((N_MSG,)), pltpu.SemaphoreType.DMA((N_MSG,)), pltpu.SemaphoreType.DMA((4,))],
        compiler_params=pltpu.CompilerParams(
            collective_id=0, has_side_effects=True, vmem_limit_bytes=56 * 2**20
        ),
        name="loss_and_block",
    )(text_emb, image_emb, groups, hidden, gain, w_in.T, w_out, w_proj)
    return pl.pallas_call(
        hand_over,
        out_shape=shapes,
        in_specs=[anywhere, anywhere],
        out_specs=(anywhere, anywhere),
        scratch_shapes=[
            pltpu.VMEM((24, E), bf16),
            pltpu.VMEM((2, 192, D), bf16),
            pltpu.VMEM((384, D), bf16),
            pltpu.SemaphoreType.DMA((10,)),
        ],
        compiler_params=pltpu.CompilerParams(vmem_limit_bytes=56 * 2**20),
        name="hand_over",
    )(*results)


def solution(mesh):
    in_specs = (
        P(("row", "col"), None),
        P(("row", "col"), None),
        P(("row", "col")),
        P("row", None),
        P(),
        P(None, "col"),
        P("col", None),
        P("col", None),
    )
    out_specs = (P(("row", "col"), None), P("row", None))
    return jax.shard_map(
        on_device, mesh=mesh, in_specs=in_specs, out_specs=out_specs, check_vma=False
    )
```

```python
import jax
import jax.numpy as jnp
from jax import lax
from jax.experimental import pallas as pl
from jax.experimental.pallas import tpu as pltpu
from jax.sharding import PartitionSpec as P

MESH = pl.DeviceIdType.MESH
bf16, f32 = jnp.bfloat16, jnp.float32
logit_scale = 0.125
eps = 1e-05
E, D, FB = 1024, 1280, 320
EX = E + 128
R2 = 48
N_MSG = 200


def device(x, y, z, c):
    x, y, z = lax.rem(x + 4, 4), lax.rem(y + 8, 8), lax.rem(z + 8, 8)
    return (z * 4 + lax.rem(y, 4), (lax.div(y, 4) * 4 + x) * 2 + c)


def rows(block, size=R2):
    return pl.ds(pl.multiple_of(block * size, 16), size)


class Net:
    def __init__(self, send_sem, recv_sem):
        self.send_sem, self.recv_sem, self.count, self.sent = send_sem, recv_sem, 0, []

    def make(self, src, dst, target):
        copy = pltpu.make_async_remote_copy(
            src_ref=src,
            dst_ref=dst,
            send_sem=self.send_sem.at[self.count],
            recv_sem=self.recv_sem.at[self.count],
            device_id=target,
            device_id_type=MESH,
        )
        self.count += 1
        return copy

    def send(self, src, dst, target):
        copy = self.make(src, dst, target)
        copy.start()
        self.sent.append(copy)
        return copy

    def finish(self):
        for copy in self.sent:
            copy.wait_send()


def nt(a, b):
    return lax.dot_general(a, b, (((1,), (1,)), ((), ())), preferred_element_type=f32)


def tn(a, b):
    return lax.dot_general(a, b, (((0,), (0,)), ((), ())), preferred_element_type=f32)


def nn(a, b):
    return jnp.dot(a, b, preferred_element_type=f32)


def log_sum_exp(parts):
    peak = parts[0]
    for part in parts[1:]:
        peak = jnp.maximum(peak, part)
    total = jnp.exp(parts[0] - peak)
    for part in parts[1:]:
        total = total + jnp.exp(part - peak)
    return peak + jnp.log(total)


def kernel(
    img_in, txt_in, grp, hid_in, gain, w_in_in, w_out_in, w_proj,
    gi_out, gh_out,
    pair_out, pair_in, both,
    img, txt, sc, pos, row_stat, ds, gi, gt, gt_sib,
    rs_out, rs_in, fin, pr_out, pr_in,
    st_r, st_c, sl_r, sl_c, st_r2, st_c2, sl_r2, sl_c2, row_b,
    slots, gtf, wp, dy, slope, part, q_in, y_out, y_in,
    hid, hid_own, wide, w_in, w_out, send_sem, recv_sem, load_sem,
):
    row, col = lax.axis_index("row"), lax.axis_index("col")
    z, yl = lax.div(row, 4), lax.rem(row, 4)
    yh, c = lax.div(col, 8), lax.rem(col, 2)
    x = lax.rem(lax.div(col, 2), 4)
    y = yh * 4 + yl
    xt = x + 1 - 2 * lax.rem(x, 2)
    xi = 3 - x
    at_t, at_i = lax.rem(x, 2), lax.div(x, 2)
    sib = device(x, y, z, 1 - c)
    part_t, part_i = device(xt, y, z, c), device(xi, y, z, c)
    part_t_sib = device(xt, y, z, 1 - c)
    y_of = [device(x, y + i, z, c) for i in range(8)]
    z_of = [device(x, y, z + i, c) for i in range(8)]
    x_of = [device(x + i, y, z, c) for i in range(4)]
    net = Net(send_sem, recv_sem)

    barrier = pltpu.get_barrier_semaphore()
    friends = y_of[1:] + z_of[1:] + x_of[1:] + [sib, part_t_sib]
    for friend in friends:
        pl.semaphore_signal(barrier, inc=1, device_id=friend, device_id_type=MESH)

    loads = [
        pltpu.make_async_copy(src, dst, load_sem.at[i])
        for i, (src, dst) in enumerate(
            ((w_proj, wp.at[rows(col, 80), :]), (hid_in, hid), (w_in_in, w_in.at[0]), (w_out_in, w_out.at[0]))
        )
    ]
    for load in loads:
        load.start()

    lane = lax.broadcasted_iota(jnp.int32, (24, 128), 1)
    line = lax.broadcasted_iota(jnp.int32, (24, 128), 0)
    ids = jnp.full((24, 128), grp[0], jnp.int32)
    for i in range(1, 24):
        ids = jnp.where(line == i, grp[i], ids)
    hit = (lane == lax.shift_right_logical(ids, 6)) | (lane == (ids & 63) + 64)
    digits = jnp.where(hit, 1.0, 0.0).astype(f32)
    own = []
    for s, ref in ((0, img_in), (1, txt_in)):
        value = jnp.concatenate([ref[...].astype(f32), digits], axis=1)
        own.append(value)
        second = jnp.concatenate([value[:, 640:], digits], axis=1)
        pair_out[s] = jnp.concatenate([value[:, :640], second], axis=0).astype(bf16)
    pl.semaphore_wait(barrier, len(friends))
    pair = [net.send(pair_out.at[s], pair_in.at[s], (part_i, part_t)[s]) for s in range(2)]

    streams = ((img, y, y_of, at_i), (txt.at[0], z, z_of, at_t))
    for s in range(2):
        buf, p, of, at = streams[s]
        both[s, pl.ds(pl.multiple_of(at * 24, 8), 24), :] = own[s]
        pair[s].wait_recv()
        other = pair_in[s].astype(f32)
        other = jnp.concatenate([other[:24], other[24:, :512]], axis=1)
        both[s, pl.ds(pl.multiple_of(24 - at * 24, 8), 24), :] = other
        buf[rows(p), :] = both[s].astype(bf16)

    gain_row = gain[...].reshape(1, D)

    def forward(i):
        halves = []
        for k in range(2):
            wide[k] = hid[pl.ds(96 * i + R2 * k, R2), :].astype(f32)
            halves.append(wide[k, pl.ds(pl.multiple_of(24 * c, 8), 24), :])
        states = jnp.concatenate(halves, axis=0)
        r = pl.ds(R2 * i, R2)
        hid_own[r, :] = states.astype(bf16)
        centered = states - jnp.mean(states, axis=1, keepdims=True)
        rstd = lax.rsqrt(jnp.mean(centered * centered, axis=1, keepdims=True) + eps)
        inner = (centered * rstd * gain_row).astype(bf16)
        for k in range(2):
            act = nt(inner, w_in[k])
            slope[k, r, :] = (
                0.5 * (1.0 + lax.erf(act * 0.7071067811865476))
                + act * jnp.exp(-0.5 * act * act) * 0.3989422804014327
            )

    ring = {}
    to_sib = []
    shards = []

    def pass_text(block):
        ref = txt.at[0, rows(block), :]
        to_sib.append(net.send(ref, txt.at[1, rows(block), :], sib))

    outer = ((2, 1, slice(0, 640)), (6, 7, slice(640, EX)))
    for s in range(2):
        buf, p, of, at = streams[s]
        block = buf.at[rows(p), :]
        for hops in (2, 6, 1, 7):
            ring[s, hops] = net.send(block, block, of[hops])
    pass_text(z)
    for s in range(2):
        buf, p, of, at = streams[s]
        for back, on, cols in outer:
            ring[s, back].wait_recv()
            origin = lax.rem(p + 8 - back, 8)
            block = buf.at[rows(origin), :]
            ring[s, "next", back] = net.send(block, block, of[on])
            block = buf.at[rows(origin), cols]
            ring[s, "far", back] = net.send(block, block, of[back])
    pass_text(lax.rem(z + 6, 8))
    pass_text(lax.rem(z + 2, 8))
    for s in range(2):
        ring[s, 1].wait_recv()
        ring[s, 7].wait_recv()
    pass_text(lax.rem(z + 7, 8))
    pass_text(lax.rem(z + 1, 8))
    for kind in ("next", "far"):
        for s in range(2):
            ring[s, kind, 2].wait_recv()
            ring[s, kind, 6].wait_recv()
        if kind == "next":
            pass_text(lax.rem(z + 5, 8))
            pass_text(lax.rem(z + 3, 8))
    pass_text(lax.rem(z + 4, 8))
    for load in loads:
        load.wait()
    weights = [net.send(w_in.at[0], w_in.at[1], sib), net.send(w_out.at[0], w_out.at[1], sib)]
    mine = wp.at[rows(col, 80), :]
    shards += [net.send(mine, mine, x_of[i]) for i in range(1, 4)]

    edge = (yl == 0) | (yl == 3)
    other_col = lax.rem(col + 8, 16)
    out_dy = jnp.where(yl == 0, -1, 1)
    theirs = wp.at[rows(other_col, 80), :]
    mine = wp.at[rows(col, 80), :]
    seam = net.make(mine, mine, device(x, y + out_dy, z, c))
    inward = pltpu.make_async_remote_copy(
        src_ref=theirs, dst_ref=theirs, send_sem=send_sem.at[N_MSG - 1], recv_sem=seam_recv(net, recv_sem),
        device_id=device(x, y - out_dy, z, c), device_id_type=MESH,
    )

    @pl.when(edge)
    def _():
        seam.start()

    first_lane = lax.broadcasted_iota(jnp.int32, (R2, 128), 1) == 0

    def tile_half(h):
        cols = slice(384 * h, 384 * h + 384)
        sc[:, cols] = logit_scale * nt(img[:, :E], txt[h, :, :E])
        pos[:, cols] = jnp.where(nt(img[:, E:], txt[h, :, E:]) > 1.5, 1.0, 0.0)

        def first_pass(i, carry):
            col_peak, col_count = carry
            r = rows(i)
            s, q = sc[r, cols], pos[r, cols]
            peak = jnp.max(s, axis=1, keepdims=True)
            lse = peak + jnp.log(jnp.sum(jnp.exp(s - peak), axis=1, keepdims=True))
            row_stat[h, r, :] = jnp.where(first_lane, lse, jnp.sum(q, axis=1, keepdims=True))
            return (
                jnp.maximum(col_peak, jnp.max(s, axis=0, keepdims=True)),
                col_count + jnp.sum(q, axis=0, keepdims=True),
            )

        col_peak, col_count = lax.fori_loop(
            0, 8, first_pass, (jnp.full((1, 384), -1e30, f32), jnp.zeros((1, 384), f32))
        )

        def second_pass(i, total):
            return total + jnp.sum(jnp.exp(sc[rows(i), cols] - col_peak), axis=0, keepdims=True)

        col_total = lax.fori_loop(0, 8, second_pass, jnp.zeros((1, 384), f32))
        st_c[0:1, cols] = col_peak + jnp.log(col_total)
        st_c[1:2, cols] = col_count

    tile_half(0)
    for copy in to_sib:
        copy.wait_recv()
    tile_half(1)
    row_stats = [row_stat[h].T[0:2, :] for h in range(2)]
    st_r[0:1, :] = log_sum_exp([v[0:1] for v in row_stats])
    st_r[1:2, :] = row_stats[0][1:2] + row_stats[1][1:2]

    sent = []
    for i in range(1, 8):
        sent.append(net.send(st_c, sl_c.at[z], z_of[i]))
        sent.append(net.send(st_r, sl_r.at[y], y_of[i]))
    sl_c[z] = st_c[...]
    sl_r[y] = st_r[...]

    seam.wait_recv()

    @pl.when(edge)
    def _():
        inward.start()

    weights[0].wait_recv()
    forward(0)
    forward(1)
    for copy in sent:
        copy.wait_recv()
    st_c2[0:1, :] = log_sum_exp([sl_c[i, 0:1, :] for i in range(8)])
    st_c2[1:2, :] = sum(sl_c[i, 1:2, :] for i in range(8))
    st_r2[0:1, :] = log_sum_exp([sl_r[i, 0:1, :] for i in range(8)])
    st_r2[1:2, :] = sum(sl_r[i, 1:2, :] for i in range(8))
    sent = [
        net.send(st_c2, sl_c2.at[0], part_t),
        net.send(st_c2, sl_c2.at[1], sib),
        net.send(st_c2, sl_c2.at[2], part_t_sib),
        net.send(st_r2, sl_r2, part_i),
    ]
    shards += [net.send(theirs, theirs, x_of[i]) for i in range(1, 4)]
    forward(2)
    forward(3)
    for copy in sent:
        copy.wait_recv()

    def swapped(value):
        return jnp.concatenate([value[:, 384:], value[:, :384]], axis=1)

    quad = [st_c2[...], sl_c2[0], swapped(sl_c2[1]), swapped(sl_c2[2])]
    col_lse = log_sum_exp([v[0:1] for v in quad])
    col_inv = 1.0 / (quad[0][1:2] + quad[1][1:2] + quad[2][1:2] + quad[3][1:2])
    row_lse = log_sum_exp([st_r2[0:1, :], sl_r2[0:1, :]])
    row_inv = 1.0 / (st_r2[1:2, :] + sl_r2[1:2, :])
    row_b[0] = jnp.broadcast_to(row_lse, (128, 384)).T
    row_b[1] = jnp.broadcast_to(row_inv, (128, 384)).T

    def dscore(i, carry):
        r = rows(i)
        s = sc[r, :]
        ds[r, :] = (
            0.5
            * (
                jnp.exp(s - row_b[0, r, 0:1])
                + jnp.exp(s - col_lse)
                - pos[r, :] * (row_b[1, r, 0:1] + col_inv)
            )
        ).astype(bf16)
        return carry

    lax.fori_loop(0, 8, dscore, 0)

    gi[...] = (
        logit_scale * (nn(ds[:, 0:384], txt[0, :, :E]) + nn(ds[:, 384:768], txt[1, :, :E]))
    ).astype(bf16)

    def term(s, block, cols):
        r = rows(block)
        if s == 0:
            return gi[r, cols].astype(f32)
        return gt[0, r, cols].astype(f32) + gt_sib[r, cols].astype(f32)

    halves = (slice(0, 512), slice(512, 1024))

    def place(s, way, far):
        p = streams[s][1]
        return lax.rem(p + far, 8) if way == 0 else lax.rem(p + 8 - far, 8)

    def hand(s, way, k, cols, value, hops):
        rs_out[s, way, k, :, cols] = value.astype(bf16)
        ring[s, way, "sum", k, cols.start] = net.send(
            rs_out.at[s, way, k, :, cols], rs_in.at[s, way, k, :, cols], streams[s][2][hops if way == 0 else 8 - hops]
        )

    def arrived(s, way, k, cols):
        ring[s, way, "sum", k, cols.start].wait_recv()
        return rs_in[s, way, k, :, cols].astype(f32)

    both_ways = (0, 1)

    def first_sums(s):
        for way in both_ways:
            hand(s, way, 1, halves[way], term(s, place(s, way, 4), halves[way]), 2)
        for h in (0, 1):
            for way in both_ways:
                cols = halves[h if way == 0 else 1 - h]
                hand(s, way, 0, cols, term(s, place(s, way, 3), cols), 1)
        for way in both_ways:
            for cols in halves:
                hand(s, way, 2, cols, term(s, place(s, way, 1), cols), 1)

    def second_sums(s):
        for h in (1, 0):
            for way in both_ways:
                cols = halves[h if way == 0 else 1 - h]
                value = term(s, place(s, way, 2), cols) + arrived(s, way, 0, cols)
                if h == 0:
                    value = value + arrived(s, way, 1, cols)
                hand(s, way, 3, cols, value, 2)

    ends = {}
    thirds = [pl.ds(16 * t, 16) for t in range(3)]

    def ring_end(s):
        p, at = streams[s][1], streams[s][3]
        for cols in halves:
            value = term(s, p, cols)
            for k in (2, 3):
                for way in both_ways:
                    value = value + arrived(s, way, k, cols)
            fin[s, :, cols] = value
        away = fin[s, pl.ds(pl.multiple_of(24 - at * 24, 8), 24), :]
        pr_out[s] = jnp.concatenate([away[:, :512], away[:, 512:]], axis=0).astype(bf16)
        for t, r in enumerate(thirds):
            ends[s, t] = net.send(pr_out.at[s, r], pr_in.at[s, r], (part_i, part_t)[s])

    def kept(s):
        at = streams[s][3]
        mine = fin[s, pl.ds(pl.multiple_of(at * 24, 8), 24), :]
        return jnp.concatenate([mine[:, :512], mine[:, 512:]], axis=0)

    first_sums(0)
    gt[1] = (logit_scale * tn(ds[:, 384:768], img[:, :E])).astype(bf16)
    half = net.send(gt.at[1], gt_sib, sib)
    gt[0] = (logit_scale * tn(ds[:, 0:384], img[:, :E])).astype(bf16)
    second_sums(0)
    half.wait_recv()
    first_sums(1)
    for copy in shards:
        copy.wait_recv()
    shards = []
    for i in range(8):
        ref = wp.at[rows(lax.rem(col + 2 * i, 16), 80), :]
        shards.append(net.send(ref, ref, sib))
    second_sums(1)
    ring_end(0)

    chip = yh * 4 + x
    other_chip = lax.rem(chip + 4, 8)
    own_text = kept(0)
    over = []
    for t, r in enumerate(thirds):
        ends[0, t].wait_recv()
        slots[chip, r, :] = (own_text[16 * t : 16 * t + 16] + pr_in[0, r, :].astype(f32)).astype(bf16)
        over.append(net.send(slots.at[chip, r], slots.at[chip, r], y_of[4]))
    near = [net.send(slots.at[chip], slots.at[chip], x_of[i]) for i in (2, 1, 3)]
    far = []
    for t, r in enumerate(thirds):
        over[t].wait_recv()
        ref = slots.at[other_chip, r]
        far += [net.send(ref, ref, x_of[i]) for i in (2, 1, 3)]
    ring_end(1)

    def lay(k, carry):
        a, b = slots[2 * k].astype(f32), slots[2 * k + 1].astype(f32)
        gtf[rows(k), 0:512] = jnp.concatenate([a[:24], b[:24]], axis=0).astype(bf16)
        gtf[rows(k), 512:1024] = jnp.concatenate([a[24:], b[24:]], axis=0).astype(bf16)
        return carry

    def block_backward(half):
        lax.fori_loop(half * 2, half * 2 + 2, lay, 0)
        r = rows(half, 96)
        dy[r, :] = nt(gtf[r, :], wp[...]).astype(bf16)
        dinner = 0.0
        for k in range(2):
            dact = (nt(dy[r, :], w_out[k]) * slope[k, r, :]).astype(bf16)
            dinner = dinner + nn(dact, w_in[k])
        part[r, :] = dinner.astype(bf16)

    weights[1].wait_recv()
    for copy in shards + near:
        copy.wait_recv()
    block_backward(yh)
    for copy in far:
        copy.wait_recv()
    block_backward(1 - yh)

    def piece(block, t):
        return pl.ds(pl.multiple_of(block * R2 + 16 * t, 16), 16)

    around = {}
    for t, r in enumerate(thirds):
        for i in (2, 1, 3):
            around[t, i] = net.send(part.at[piece(lax.rem(x + i, 4), t), :], q_in.at[i - 1, r], x_of[i])
    for t in range(3):
        ends[1, t].wait_recv()
    final_image = kept(1) + pr_in[1].astype(f32)
    gi_out[...] = jnp.concatenate([final_image[:24], final_image[24:]], axis=1).astype(bf16)
    over = []
    for t, r in enumerate(thirds):
        total = part[piece(x, t), :].astype(f32)
        for i in (1, 3, 2):
            around[t, i].wait_recv()
            total = total + q_in[i - 1, r, :].astype(f32)
        y_out[r, :] = total.astype(bf16)
        over.append(net.send(y_out.at[r], y_in.at[r], y_of[4]))

    to_sib = []
    for t, r in enumerate(thirds):
        mine = piece(x, t)
        states = hid_own[mine, :].astype(f32)
        centered = states - jnp.mean(states, axis=1, keepdims=True)
        rstd = lax.rsqrt(jnp.mean(centered * centered, axis=1, keepdims=True) + eps)
        normed = centered * rstd
        over[t].wait_recv()
        scaled = (y_out[r, :].astype(f32) + y_in[r, :].astype(f32)) * gain_row
        back = rstd * (
            scaled
            - jnp.mean(scaled, axis=1, keepdims=True)
            - normed * jnp.mean(scaled * normed, axis=1, keepdims=True)
        )
        gh_out[c, mine, :] = (dy[mine, :].astype(f32) + back).astype(bf16)
        ref = gh_out.at[c, mine, :]
        for i in (2, 1, 3):
            around[t, i] = net.send(ref, ref, x_of[i])
        to_sib.append(net.send(ref, ref, sib))
    for t in range(3):
        for i in (1, 3, 2):
            around[t, i].wait_recv()
            ref = gh_out.at[c, piece(lax.rem(x + 4 - i, 4), t), :]
            to_sib.append(net.send(ref, ref, sib))
    for copy in to_sib:
        copy.wait_recv()
    net.finish()

    @pl.when(edge)
    def _():
        seam.wait_send()
        inward.wait_send()


def seam_recv(net, recv_sem):
    return recv_sem.at[net.count - 1]


def hand_over(gi, gh, gi_out, gh_out, gi_held, held, laid, sem):
    pieces = [pl.ds(R2 * i, R2) for i in range(4)]
    reads = [pltpu.make_async_copy(gh.at[:, p], held.at[:, p], sem.at[i]) for i, p in enumerate(pieces)]
    first = pltpu.make_async_copy(gi, gi_held, sem.at[4])
    last = pltpu.make_async_copy(gi_held, gi_out, sem.at[5])
    first.start()
    for copy in reads:
        copy.start()
    first.wait()
    last.start()
    writes = []
    for i, p in enumerate(pieces):
        reads[i].wait()
        a, b = held[0, p, :].astype(f32), held[1, p, :].astype(f32)
        out = pl.ds(96 * i, 96)
        laid[out, :] = jnp.concatenate([a[:24], b[:24], a[24:], b[24:]], axis=0).astype(bf16)
        writes.append(pltpu.make_async_copy(laid.at[out], gh_out.at[out], sem.at[6 + i]))
        writes[i].start()
    for copy in writes + [last]:
        copy.wait()


def on_device(image_emb, text_emb, groups, hidden, gain, w_in, w_out, w_proj):
    vmem = pl.BlockSpec(memory_space=pltpu.VMEM)
    shapes = (jax.ShapeDtypeStruct((24, E), bf16), jax.ShapeDtypeStruct((384, D), bf16))
    scratch = [
        ((2, R2, 640), bf16), ((2, R2, 640), bf16), ((2, R2, EX), f32),
        ((384, EX), bf16), ((2, 384, EX), bf16), ((384, 768), f32), ((384, 768), f32), ((2, 384, 128), f32),
        ((384, 768), bf16), ((384, E), bf16), ((2, 384, E), bf16), ((384, E), bf16),
        ((2, 2, 4, R2, E), bf16), ((2, 2, 4, R2, E), bf16), ((2, R2, E), f32), ((2, R2, 512), bf16), ((2, R2, 512), bf16),
        ((2, 384), f32), ((2, 768), f32), ((8, 2, 384), f32), ((8, 2, 768), f32),
        ((2, 384), f32), ((2, 768), f32), ((2, 384), f32), ((3, 2, 768), f32), ((2, 384, 128), f32),
        ((8, R2, 512), bf16), ((192, E), bf16), ((D, E), bf16), ((192, D), bf16), ((2, 192, FB), f32),
        ((192, D), bf16), ((3, R2, D), bf16), ((R2, D), bf16), ((R2, D), bf16),
        ((384, D), bf16), ((192, D), bf16), ((2, R2, D), f32), ((2, FB, D), bf16), ((2, FB, D), bf16),
    ]
    anywhere = pl.BlockSpec(memory_space=pl.ANY)
    results = pl.pallas_call(
        kernel,
        out_shape=(shapes[0], jax.ShapeDtypeStruct((2, 192, D), bf16)),
        in_specs=[vmem, vmem, pl.BlockSpec(memory_space=pltpu.SMEM), anywhere, vmem] + [anywhere] * 3,
        out_specs=(vmem, vmem),
        scratch_shapes=[pltpu.VMEM(shape, dtype) for shape, dtype in scratch]
        + [pltpu.SemaphoreType.DMA((N_MSG,)), pltpu.SemaphoreType.DMA((N_MSG,)), pltpu.SemaphoreType.DMA((4,))],
        compiler_params=pltpu.CompilerParams(
            collective_id=0, has_side_effects=True, vmem_limit_bytes=56 * 2**20
        ),
        name="loss_and_block",
    )(text_emb, image_emb, groups, hidden, gain, w_in.T, w_out, w_proj)
    return pl.pallas_call(
        hand_over,
        out_shape=shapes,
        in_specs=[anywhere, anywhere],
        out_specs=(anywhere, anywhere),
        scratch_shapes=[
            pltpu.VMEM((24, E), bf16),
            pltpu.VMEM((2, 192, D), bf16),
            pltpu.VMEM((384, D), bf16),
            pltpu.SemaphoreType.DMA((10,)),
        ],
        compiler_params=pltpu.CompilerParams(vmem_limit_bytes=56 * 2**20),
        name="hand_over",
    )(*results)


def solution(mesh):
    in_specs = (
        P(("row", "col"), None),
        P(("row", "col"), None),
        P(("row", "col")),
        P("row", None),
        P(),
        P(None, "col"),
        P("col", None),
        P("col", None),
    )
    out_specs = (P(("row", "col"), None), P("row", None))
    return jax.shard_map(
        on_device, mesh=mesh, in_specs=in_specs, out_specs=out_specs, check_vma=False
    )
```

```python
import jax
import jax.numpy as jnp
from jax import lax
from jax.experimental import pallas as pl
from jax.experimental.pallas import tpu as pltpu
from jax.sharding import PartitionSpec as P

MESH = pl.DeviceIdType.MESH
bf16, f32 = jnp.bfloat16, jnp.float32
logit_scale = 0.125
eps = 1e-05
E, D, FB = 1024, 1280, 320
EX = E + 128
R2 = 48
N_MSG = 200


def device(x, y, z, c):
    x, y, z = lax.rem(x + 4, 4), lax.rem(y + 8, 8), lax.rem(z + 8, 8)
    return (z * 4 + lax.rem(y, 4), (lax.div(y, 4) * 4 + x) * 2 + c)


def rows(block, size=R2):
    return pl.ds(pl.multiple_of(block * size, 16), size)


class Net:
    def __init__(self, send_sem, recv_sem):
        self.send_sem, self.recv_sem, self.count, self.sent = send_sem, recv_sem, 0, []

    def make(self, src, dst, target):
        copy = pltpu.make_async_remote_copy(
            src_ref=src,
            dst_ref=dst,
            send_sem=self.send_sem.at[self.count],
            recv_sem=self.recv_sem.at[self.count],
            device_id=target,
            device_id_type=MESH,
        )
        self.count += 1
        return copy

    def send(self, src, dst, target):
        copy = self.make(src, dst, target)
        copy.start()
        self.sent.append(copy)
        return copy

    def settle(self, copies):
        for copy in copies:
            copy.wait_send()
        self.sent = [copy for copy in self.sent if not any(copy is done for done in copies)]

    def finish(self):
        self.settle(self.sent)


def nt(a, b):
    return lax.dot_general(a, b, (((1,), (1,)), ((), ())), preferred_element_type=f32)


def tn(a, b):
    return lax.dot_general(a, b, (((0,), (0,)), ((), ())), preferred_element_type=f32)


def nn(a, b):
    return jnp.dot(a, b, preferred_element_type=f32)


def log_sum_exp(parts):
    peak = parts[0]
    for part in parts[1:]:
        peak = jnp.maximum(peak, part)
    total = jnp.exp(parts[0] - peak)
    for part in parts[1:]:
        total = total + jnp.exp(part - peak)
    return peak + jnp.log(total)


def kernel(
    img_in, txt_in, grp, hid_in, gain, w_in_in, w_out_in, w_proj,
    gi_out, gh_out,
    pair_out, pair_in, both,
    img, txt, sc, pos, row_stat, ds, gi, gt, gt_sib,
    rs_out, rs_in, fin, pr_out, pr_in,
    st_r, st_c, sl_r, sl_c, st_r2, st_c2, sl_r2, sl_c2, row_b,
    slots, gtf, wp, dy, slope, part, q_in, y_out, y_in,
    hid, hid_own, wide, w_in, w_out, send_sem, recv_sem, load_sem,
):
    row, col = lax.axis_index("row"), lax.axis_index("col")
    z, yl = lax.div(row, 4), lax.rem(row, 4)
    yh, c = lax.div(col, 8), lax.rem(col, 2)
    x = lax.rem(lax.div(col, 2), 4)
    y = yh * 4 + yl
    xt = x + 1 - 2 * lax.rem(x, 2)
    xi = 3 - x
    at_t, at_i = lax.rem(x, 2), lax.div(x, 2)
    sib = device(x, y, z, 1 - c)
    part_t, part_i = device(xt, y, z, c), device(xi, y, z, c)
    part_t_sib = device(xt, y, z, 1 - c)
    y_of = [device(x, y + i, z, c) for i in range(8)]
    z_of = [device(x, y, z + i, c) for i in range(8)]
    x_of = [device(x + i, y, z, c) for i in range(4)]
    net = Net(send_sem, recv_sem)

    barrier = pltpu.get_barrier_semaphore()
    friends = y_of[1:] + z_of[1:] + x_of[1:] + [sib, part_t_sib]
    for friend in friends:
        pl.semaphore_signal(barrier, inc=1, device_id=friend, device_id_type=MESH)

    loads = [
        pltpu.make_async_copy(src, dst, load_sem.at[i])
        for i, (src, dst) in enumerate(
            ((w_proj, wp.at[rows(col, 80), :]), (hid_in, hid), (w_in_in, w_in.at[0]), (w_out_in, w_out.at[0]))
        )
    ]
    for load in loads:
        load.start()

    lane = lax.broadcasted_iota(jnp.int32, (24, 128), 1)
    line = lax.broadcasted_iota(jnp.int32, (24, 128), 0)
    ids = jnp.full((24, 128), grp[0], jnp.int32)
    for i in range(1, 24):
        ids = jnp.where(line == i, grp[i], ids)
    hit = (lane == lax.shift_right_logical(ids, 6)) | (lane == (ids & 63) + 64)
    digits = jnp.where(hit, 1.0, 0.0).astype(f32)
    own = []
    for s, ref in ((0, img_in), (1, txt_in)):
        value = jnp.concatenate([ref[...].astype(f32), digits], axis=1)
        own.append(value)
        second = jnp.concatenate([value[:, 640:], digits], axis=1)
        pair_out[s] = jnp.concatenate([value[:, :640], second], axis=0).astype(bf16)
    pl.semaphore_wait(barrier, len(friends))
    pair = [net.send(pair_out.at[s], pair_in.at[s], (part_i, part_t)[s]) for s in range(2)]

    streams = ((img, y, y_of, at_i), (txt.at[0], z, z_of, at_t))
    for s in range(2):
        buf, p, of, at = streams[s]
        both[s, pl.ds(pl.multiple_of(at * 24, 8), 24), :] = own[s]
        pair[s].wait_recv()
        other = pair_in[s].astype(f32)
        other = jnp.concatenate([other[:24], other[24:, :512]], axis=1)
        both[s, pl.ds(pl.multiple_of(24 - at * 24, 8), 24), :] = other
        buf[rows(p), :] = both[s].astype(bf16)

    gain_row = gain[...].reshape(1, D)

    def forward(i):
        halves = []
        for k in range(2):
            wide[k] = hid[pl.ds(96 * i + R2 * k, R2), :].astype(f32)
            halves.append(wide[k, pl.ds(pl.multiple_of(24 * c, 8), 24), :])
        states = jnp.concatenate(halves, axis=0)
        r = pl.ds(R2 * i, R2)
        hid_own[r, :] = states.astype(bf16)
        centered = states - jnp.mean(states, axis=1, keepdims=True)
        rstd = lax.rsqrt(jnp.mean(centered * centered, axis=1, keepdims=True) + eps)
        inner = (centered * rstd * gain_row).astype(bf16)
        for k in range(2):
            act = nt(inner, w_in[k])
            slope[k, r, :] = (
                0.5 * (1.0 + lax.erf(act * 0.7071067811865476))
                + act * jnp.exp(-0.5 * act * act) * 0.3989422804014327
            )

    ring = {}
    to_sib = []
    shards = []

    def pass_text(block):
        ref = txt.at[0, rows(block), :]
        to_sib.append(net.send(ref, txt.at[1, rows(block), :], sib))

    outer = ((2, 1, slice(0, 640)), (6, 7, slice(640, EX)))
    for s in range(2):
        buf, p, of, at = streams[s]
        block = buf.at[rows(p), :]
        for hops in (2, 6, 1, 7):
            ring[s, hops] = net.send(block, block, of[hops])
    pass_text(z)
    for s in range(2):
        buf, p, of, at = streams[s]
        for back, on, cols in outer:
            ring[s, back].wait_recv()
            origin = lax.rem(p + 8 - back, 8)
            block = buf.at[rows(origin), :]
            ring[s, "next", back] = net.send(block, block, of[on])
            block = buf.at[rows(origin), cols]
            ring[s, "far", back] = net.send(block, block, of[back])
    pass_text(lax.rem(z + 6, 8))
    pass_text(lax.rem(z + 2, 8))
    for s in range(2):
        ring[s, 1].wait_recv()
        ring[s, 7].wait_recv()
    pass_text(lax.rem(z + 7, 8))
    pass_text(lax.rem(z + 1, 8))
    for kind in ("next", "far"):
        for s in range(2):
            ring[s, kind, 2].wait_recv()
            ring[s, kind, 6].wait_recv()
        if kind == "next":
            pass_text(lax.rem(z + 5, 8))
            pass_text(lax.rem(z + 3, 8))
    pass_text(lax.rem(z + 4, 8))
    gather_sends = list(net.sent)
    for load in loads:
        load.wait()
    weights = [net.send(w_in.at[0], w_in.at[1], sib), net.send(w_out.at[0], w_out.at[1], sib)]
    mine = wp.at[rows(col, 80), :]
    shards += [net.send(mine, mine, x_of[i]) for i in range(1, 4)]

    edge = (yl == 0) | (yl == 3)
    other_col = lax.rem(col + 8, 16)
    out_dy = jnp.where(yl == 0, -1, 1)
    theirs = wp.at[rows(other_col, 80), :]
    mine = wp.at[rows(col, 80), :]
    seam = net.make(mine, mine, device(x, y + out_dy, z, c))
    inward = pltpu.make_async_remote_copy(
        src_ref=theirs, dst_ref=theirs, send_sem=send_sem.at[N_MSG - 1], recv_sem=seam_recv(net, recv_sem),
        device_id=device(x, y - out_dy, z, c), device_id_type=MESH,
    )

    @pl.when(edge)
    def _():
        seam.start()

    first_lane = lax.broadcasted_iota(jnp.int32, (R2, 128), 1) == 0

    def tile_half(h):
        cols = slice(384 * h, 384 * h + 384)
        sc[:, cols] = logit_scale * nt(img[:, :E], txt[h, :, :E])
        pos[:, cols] = jnp.where(nt(img[:, E:], txt[h, :, E:]) > 1.5, 1.0, 0.0)

        def first_pass(i, carry):
            col_peak, col_count = carry
            r = rows(i)
            s, q = sc[r, cols], pos[r, cols]
            peak = jnp.max(s, axis=1, keepdims=True)
            lse = peak + jnp.log(jnp.sum(jnp.exp(s - peak), axis=1, keepdims=True))
            row_stat[h, r, :] = jnp.where(first_lane, lse, jnp.sum(q, axis=1, keepdims=True))
            return (
                jnp.maximum(col_peak, jnp.max(s, axis=0, keepdims=True)),
                col_count + jnp.sum(q, axis=0, keepdims=True),
            )

        col_peak, col_count = lax.fori_loop(
            0, 8, first_pass, (jnp.full((1, 384), -1e30, f32), jnp.zeros((1, 384), f32)), unroll=2
        )

        def second_pass(i, total):
            return total + jnp.sum(jnp.exp(sc[rows(i), cols] - col_peak), axis=0, keepdims=True)

        col_total = lax.fori_loop(0, 8, second_pass, jnp.zeros((1, 384), f32))
        st_c[0:1, cols] = col_peak + jnp.log(col_total)
        st_c[1:2, cols] = col_count

    tile_half(0)
    for copy in to_sib:
        copy.wait_recv()
    tile_half(1)
    row_stats = [row_stat[h].T[0:2, :] for h in range(2)]
    st_r[0:1, :] = log_sum_exp([v[0:1] for v in row_stats])
    st_r[1:2, :] = row_stats[0][1:2] + row_stats[1][1:2]

    sent = []
    for i in range(1, 8):
        sent.append(net.send(st_c, sl_c.at[z], z_of[i]))
        sent.append(net.send(st_r, sl_r.at[y], y_of[i]))
    sl_c[z] = st_c[...]
    sl_r[y] = st_r[...]

    seam.wait_recv()

    @pl.when(edge)
    def _():
        inward.start()

    weights[0].wait_recv()
    forward(0)
    forward(1)
    net.settle(gather_sends)
    for copy in sent:
        copy.wait_recv()
    st_c2[0:1, :] = log_sum_exp([sl_c[i, 0:1, :] for i in range(8)])
    st_c2[1:2, :] = sum(sl_c[i, 1:2, :] for i in range(8))
    st_r2[0:1, :] = log_sum_exp([sl_r[i, 0:1, :] for i in range(8)])
    st_r2[1:2, :] = sum(sl_r[i, 1:2, :] for i in range(8))
    sent = [
        net.send(st_c2, sl_c2.at[0], part_t),
        net.send(st_c2, sl_c2.at[1], sib),
        net.send(st_c2, sl_c2.at[2], part_t_sib),
        net.send(st_r2, sl_r2, part_i),
    ]
    shards += [net.send(theirs, theirs, x_of[i]) for i in range(1, 4)]
    forward(2)
    forward(3)
    for copy in sent:
        copy.wait_recv()

    def swapped(value):
        return jnp.concatenate([value[:, 384:], value[:, :384]], axis=1)

    quad = [st_c2[...], sl_c2[0], swapped(sl_c2[1]), swapped(sl_c2[2])]
    col_lse = log_sum_exp([v[0:1] for v in quad])
    col_inv = 1.0 / (quad[0][1:2] + quad[1][1:2] + quad[2][1:2] + quad[3][1:2])
    row_lse = log_sum_exp([st_r2[0:1, :], sl_r2[0:1, :]])
    row_inv = 1.0 / (st_r2[1:2, :] + sl_r2[1:2, :])
    row_b[0] = jnp.broadcast_to(row_lse, (128, 384)).T
    row_b[1] = jnp.broadcast_to(row_inv, (128, 384)).T

    def dscore(i, carry):
        r = rows(i)
        s = sc[r, :]
        ds[r, :] = (
            0.5
            * (
                jnp.exp(s - row_b[0, r, 0:1])
                + jnp.exp(s - col_lse)
                - pos[r, :] * (row_b[1, r, 0:1] + col_inv)
            )
        ).astype(bf16)
        return carry

    lax.fori_loop(0, 8, dscore, 0)

    gi[...] = (
        logit_scale * (nn(ds[:, 0:384], txt[0, :, :E]) + nn(ds[:, 384:768], txt[1, :, :E]))
    ).astype(bf16)

    def term(s, block, cols):
        r = rows(block)
        if s == 0:
            return gi[r, cols].astype(f32)
        return gt[0, r, cols].astype(f32) + gt_sib[r, cols].astype(f32)

    halves = (slice(0, 512), slice(512, 1024))

    def place(s, way, far):
        p = streams[s][1]
        return lax.rem(p + far, 8) if way == 0 else lax.rem(p + 8 - far, 8)

    def hand(s, way, k, cols, value, hops):
        rs_out[s, way, k, :, cols] = value.astype(bf16)
        ring[s, way, "sum", k, cols.start] = net.send(
            rs_out.at[s, way, k, :, cols], rs_in.at[s, way, k, :, cols], streams[s][2][hops if way == 0 else 8 - hops]
        )

    def arrived(s, way, k, cols):
        ring[s, way, "sum", k, cols.start].wait_recv()
        return rs_in[s, way, k, :, cols].astype(f32)

    both_ways = (0, 1)

    def first_sums(s):
        for way in both_ways:
            hand(s, way, 1, halves[way], term(s, place(s, way, 4), halves[way]), 2)
        for h in (0, 1):
            for way in both_ways:
                cols = halves[h if way == 0 else 1 - h]
                hand(s, way, 0, cols, term(s, place(s, way, 3), cols), 1)
        for way in both_ways:
            for cols in halves:
                hand(s, way, 2, cols, term(s, place(s, way, 1), cols), 1)

    def second_sums(s):
        for h in (1, 0):
            for way in both_ways:
                cols = halves[h if way == 0 else 1 - h]
                value = term(s, place(s, way, 2), cols) + arrived(s, way, 0, cols)
                if h == 0:
                    value = value + arrived(s, way, 1, cols)
                hand(s, way, 3, cols, value, 2)

    ends = {}
    thirds = [pl.ds(16 * t, 16) for t in range(3)]

    def ring_end(s):
        p, at = streams[s][1], streams[s][3]
        for cols in halves:
            value = term(s, p, cols)
            for k in (2, 3):
                for way in both_ways:
                    value = value + arrived(s, way, k, cols)
            fin[s, :, cols] = value
        away = fin[s, pl.ds(pl.multiple_of(24 - at * 24, 8), 24), :]
        pr_out[s] = jnp.concatenate([away[:, :512], away[:, 512:]], axis=0).astype(bf16)
        for t, r in enumerate(thirds):
            ends[s, t] = net.send(pr_out.at[s, r], pr_in.at[s, r], (part_i, part_t)[s])

    def kept(s):
        at = streams[s][3]
        mine = fin[s, pl.ds(pl.multiple_of(at * 24, 8), 24), :]
        return jnp.concatenate([mine[:, :512], mine[:, 512:]], axis=0)

    middle_sends = list(net.sent)
    first_sums(0)
    gt[1] = (logit_scale * tn(ds[:, 384:768], img[:, :E])).astype(bf16)
    half = net.send(gt.at[1], gt_sib, sib)
    gt[0] = (logit_scale * tn(ds[:, 0:384], img[:, :E])).astype(bf16)
    second_sums(0)
    half.wait_recv()
    first_sums(1)
    for copy in shards:
        copy.wait_recv()
    shards = []
    for i in range(8):
        ref = wp.at[rows(lax.rem(col + 2 * i, 16), 80), :]
        shards.append(net.send(ref, ref, sib))
    second_sums(1)
    ring_end(0)

    chip = yh * 4 + x
    other_chip = lax.rem(chip + 4, 8)
    own_text = kept(0)
    over = []
    for t, r in enumerate(thirds):
        ends[0, t].wait_recv()
        slots[chip, r, :] = (own_text[16 * t : 16 * t + 16] + pr_in[0, r, :].astype(f32)).astype(bf16)
        over.append(net.send(slots.at[chip, r], slots.at[chip, r], y_of[4]))
    near = [net.send(slots.at[chip], slots.at[chip], x_of[i]) for i in (2, 1, 3)]
    net.settle(middle_sends)
    far = []
    for t, r in enumerate(thirds):
        over[t].wait_recv()
        ref = slots.at[other_chip, r]
        far += [net.send(ref, ref, x_of[i]) for i in (2, 1, 3)]
    ring_end(1)

    def lay(k, carry):
        a, b = slots[2 * k].astype(f32), slots[2 * k + 1].astype(f32)
        gtf[rows(k), 0:512] = jnp.concatenate([a[:24], b[:24]], axis=0).astype(bf16)
        gtf[rows(k), 512:1024] = jnp.concatenate([a[24:], b[24:]], axis=0).astype(bf16)
        return carry

    def block_backward(half):
        lax.fori_loop(half * 2, half * 2 + 2, lay, 0)
        r = rows(half, 96)
        dy[r, :] = nt(gtf[r, :], wp[...]).astype(bf16)
        dinner = 0.0
        for k in range(2):
            dact = (nt(dy[r, :], w_out[k]) * slope[k, r, :]).astype(bf16)
            dinner = dinner + nn(dact, w_in[k])
        part[r, :] = dinner.astype(bf16)

    weights[1].wait_recv()
    for copy in shards + near:
        copy.wait_recv()
    block_backward(yh)
    for copy in far:
        copy.wait_recv()
    block_backward(1 - yh)

    def piece(block, t):
        return pl.ds(pl.multiple_of(block * R2 + 16 * t, 16), 16)

    sum_sends = list(net.sent)
    around = {}
    for t, r in enumerate(thirds):
        for i in (2, 1, 3):
            around[t, i] = net.send(part.at[piece(lax.rem(x + i, 4), t), :], q_in.at[i - 1, r], x_of[i])
    for t in range(3):
        ends[1, t].wait_recv()
    final_image = kept(1) + pr_in[1].astype(f32)
    gi_out[...] = jnp.concatenate([final_image[:24], final_image[24:]], axis=1).astype(bf16)
    net.settle(sum_sends)
    dinner_sends = list(net.sent)
    over = []
    for t, r in enumerate(thirds):
        total = part[piece(x, t), :].astype(f32)
        for i in (1, 3, 2):
            around[t, i].wait_recv()
            total = total + q_in[i - 1, r, :].astype(f32)
        y_out[r, :] = total.astype(bf16)
        over.append(net.send(y_out.at[r], y_in.at[r], y_of[4]))

    net.settle(dinner_sends)
    to_sib = []
    for t, r in enumerate(thirds):
        mine = piece(x, t)
        states = hid_own[mine, :].astype(f32)
        centered = states - jnp.mean(states, axis=1, keepdims=True)
        rstd = lax.rsqrt(jnp.mean(centered * centered, axis=1, keepdims=True) + eps)
        normed = centered * rstd
        over[t].wait_recv()
        scaled = (y_out[r, :].astype(f32) + y_in[r, :].astype(f32)) * gain_row
        back = rstd * (
            scaled
            - jnp.mean(scaled, axis=1, keepdims=True)
            - normed * jnp.mean(scaled * normed, axis=1, keepdims=True)
        )
        gh_out[c, mine, :] = (dy[mine, :].astype(f32) + back).astype(bf16)
        ref = gh_out.at[c, mine, :]
        for i in (2, 1, 3):
            around[t, i] = net.send(ref, ref, x_of[i])
        to_sib.append(net.send(ref, ref, sib))
    for t in range(3):
        for i in (1, 3, 2):
            around[t, i].wait_recv()
            ref = gh_out.at[c, piece(lax.rem(x + 4 - i, 4), t), :]
            to_sib.append(net.send(ref, ref, sib))
    for copy in to_sib:
        copy.wait_recv()
    net.finish()

    @pl.when(edge)
    def _():
        seam.wait_send()
        inward.wait_send()


def seam_recv(net, recv_sem):
    return recv_sem.at[net.count - 1]


def hand_over(gi, gh, gi_out, gh_out, gi_held, held, laid, sem):
    pieces = [pl.ds(R2 * i, R2) for i in range(4)]
    reads = [pltpu.make_async_copy(gh.at[:, p], held.at[:, p], sem.at[i]) for i, p in enumerate(pieces)]
    first = pltpu.make_async_copy(gi, gi_held, sem.at[4])
    last = pltpu.make_async_copy(gi_held, gi_out, sem.at[5])
    first.start()
    for copy in reads:
        copy.start()
    first.wait()
    last.start()
    writes = []
    for i, p in enumerate(pieces):
        reads[i].wait()
        a, b = held[0, p, :].astype(f32), held[1, p, :].astype(f32)
        out = pl.ds(96 * i, 96)
        laid[out, :] = jnp.concatenate([a[:24], b[:24], a[24:], b[24:]], axis=0).astype(bf16)
        writes.append(pltpu.make_async_copy(laid.at[out], gh_out.at[out], sem.at[6 + i]))
        writes[i].start()
    for copy in writes + [last]:
        copy.wait()


def on_device(image_emb, text_emb, groups, hidden, gain, w_in, w_out, w_proj):
    vmem = pl.BlockSpec(memory_space=pltpu.VMEM)
    shapes = (jax.ShapeDtypeStruct((24, E), bf16), jax.ShapeDtypeStruct((384, D), bf16))
    scratch = [
        ((2, R2, 640), bf16), ((2, R2, 640), bf16), ((2, R2, EX), f32),
        ((384, EX), bf16), ((2, 384, EX), bf16), ((384, 768), f32), ((384, 768), f32), ((2, 384, 128), f32),
        ((384, 768), bf16), ((384, E), bf16), ((2, 384, E), bf16), ((384, E), bf16),
        ((2, 2, 4, R2, E), bf16), ((2, 2, 4, R2, E), bf16), ((2, R2, E), f32), ((2, R2, 512), bf16), ((2, R2, 512), bf16),
        ((2, 384), f32), ((2, 768), f32), ((8, 2, 384), f32), ((8, 2, 768), f32),
        ((2, 384), f32), ((2, 768), f32), ((2, 384), f32), ((3, 2, 768), f32), ((2, 384, 128), f32),
        ((8, R2, 512), bf16), ((192, E), bf16), ((D, E), bf16), ((192, D), bf16), ((2, 192, FB), f32),
        ((192, D), bf16), ((3, R2, D), bf16), ((R2, D), bf16), ((R2, D), bf16),
        ((384, D), bf16), ((192, D), bf16), ((2, R2, D), f32), ((2, FB, D), bf16), ((2, FB, D), bf16),
    ]
    anywhere = pl.BlockSpec(memory_space=pl.ANY)
    results = pl.pallas_call(
        kernel,
        out_shape=(shapes[0], jax.ShapeDtypeStruct((2, 192, D), bf16)),
        in_specs=[vmem, vmem, pl.BlockSpec(memory_space=pltpu.SMEM), anywhere, vmem] + [anywhere] * 3,
        out_specs=(vmem, vmem),
        scratch_shapes=[pltpu.VMEM(shape, dtype) for shape, dtype in scratch]
        + [pltpu.SemaphoreType.DMA((N_MSG,)), pltpu.SemaphoreType.DMA((N_MSG,)), pltpu.SemaphoreType.DMA((4,))],
        compiler_params=pltpu.CompilerParams(
            collective_id=0, has_side_effects=True, vmem_limit_bytes=56 * 2**20
        ),
        name="loss_and_block",
    )(text_emb, image_emb, groups, hidden, gain, w_in.T, w_out, w_proj)
    return pl.pallas_call(
        hand_over,
        out_shape=shapes,
        in_specs=[anywhere, anywhere],
        out_specs=(anywhere, anywhere),
        scratch_shapes=[
            pltpu.VMEM((24, E), bf16),
            pltpu.VMEM((2, 192, D), bf16),
            pltpu.VMEM((384, D), bf16),
            pltpu.SemaphoreType.DMA((10,)),
        ],
        compiler_params=pltpu.CompilerParams(vmem_limit_bytes=56 * 2**20),
        name="hand_over",
    )(*results)


def solution(mesh):
    in_specs = (
        P(("row", "col"), None),
        P(("row", "col"), None),
        P(("row", "col")),
        P("row", None),
        P(),
        P(None, "col"),
        P("col", None),
        P("col", None),
    )
    out_specs = (P(("row", "col"), None), P("row", None))
    return jax.shard_map(
        on_device, mesh=mesh, in_specs=in_specs, out_specs=out_specs, check_vma=False
    )
```
